256 devices in a mesh: aux: 32 (over y, z), orb: 4 (over x_hi, core), rdm: 2 (over x_lo).
Axes of the slice: x: 4 (x_hi: 2, x_lo: 2; x = x_hi * 2 + x_lo), y: 4, z: 8, core: 2. Of those that a mesh axis runs over, the one named last changes fastest.
Arguments:
- pair_coeffs: float32 [1536, 9216], P('aux', ('orb', 'rdm')), may hold values from -6 to 6
- rdm: float32 [9216, 9216], P('aux', ('orb', 'rdm')), may hold values from -0.625 to 0.625
- b_tensor: float32 [1536, 96, 4000], P('aux', None, ('orb', 'rdm')), may hold values from -4.6875 to 4.6875
- gen_coeffs: float32 [4000, 4000], P('aux', ('orb', 'rdm')), may hold values from -6 to 6
- act_coeffs: float32 [4000, 96], P('aux'), may hold values from -38.418747 to 38.418747
Outputs:
- direction: float32 [96, 4000], P(None, ('orb', 'rdm'))
- active_shift: float32 [4000, 96], P('aux')
- general_shift: float32 [4000, 4000], P('aux', ('orb', 'rdm'))
The draws below stay inside these ranges and needn't reach their ends.
All inputs are finite; a program needn't handle non-finite values.
Results may differ from the reference program's by a relative error of at most 0.0001.
Values sent between devices are 32-bit elements; how exact they have to be, the bound alone decides.
No kernel may reach another device: no remote copies, remote signals or barrier semaphores. Data moves between devices by JAX's collectives and lax.ppermute only.
A program may use at most 64 MiB of HBM per device.

```python
import jax
import jax.numpy as jnp
from jax import lax

AUX_DEV = 48
NACT = 96
NORB = 4000
NBAS = 4000
NAUX = 1536
NPAIR = 9216
N_AUX = 32


def draw_rdm(key, part):
    key = jax.random.fold_in(key, 12)
    first, second = jax.random.split(key, 2)
    base = jnp.clip(jax.random.normal(first, (NPAIR, NPAIR)), -6.0, 6.0)
    scales = 10.0 ** jax.random.uniform(second, (NPAIR, 1))
    return (base * scales / jnp.sqrt(jnp.float32(NPAIR))).astype(jnp.float32)


def draw_b_tensor(key, part):
    key = jax.random.fold_in(key, 11)
    first, second, third = jax.random.split(key, 3)
    columns = 3.0 ** (jnp.arange(NORB, dtype=jnp.float32) / NORB) * 10.0 ** jax.random.uniform(second, (NORB,))
    rows_scale = 10.0 ** jax.random.uniform(third, (NACT, 1))
    base = jnp.clip(jax.random.normal(first, (NAUX, NACT, NORB)), -6.0, 6.0)
    return (base * rows_scale * columns / jnp.sqrt(jnp.float32(NAUX * NACT))).astype(jnp.float32)


def levels(rng, extent, cuts, low, high):
    level = 1.0
    for dim, shards_of in cuts:
        draws = jax.random.uniform(jax.random.fold_in(jax.random.fold_in(rng, 6), dim), (shards_of,), jnp.float32, low / len(cuts), high / len(cuts))
        level = level * jnp.repeat(jnp.exp(draws), extent[dim] // shards_of).reshape((-1,) + (1,) * (len(extent) - 1 - dim))
    return level


def gaussian(rng, shape, spread, bound, cuts=(), kind=jnp.bfloat16):
    loudness = levels(rng, shape, cuts, -0.22, 0.18) if cuts else 1.0
    entries = jax.random.normal(rng, shape, jnp.float32) * spread * loudness
    return jnp.minimum(jnp.maximum(entries, -bound), bound).astype(kind)


def setup_inputs(seed: int = 0) -> dict:
    seeds = jax.random.split(jax.random.key(seed), 6)
    pair_coeffs = gaussian(seeds[0], (NAUX, NPAIR), 1.0, 6.0, ((0, 32), (1, 8)), jnp.float32)
    rdm = draw_rdm(jax.random.fold_in(seeds[5], 71), 0)
    b_tensor = draw_b_tensor(jax.random.fold_in(seeds[5], 71), 0)
    gen_coeffs = gaussian(seeds[3], (NBAS, NORB), 1.0, 6.0, ((0, 32), (1, 8)), jnp.float32)
    act_coeffs = gaussian(seeds[4], (NBAS, NACT), ((NORB // NACT) ** 0.5), 38.418747, ((0, 32),), jnp.float32)
    return {"pair_coeffs": pair_coeffs, "rdm": rdm, "b_tensor": b_tensor, "gen_coeffs": gen_coeffs, "act_coeffs": act_coeffs}


def reference(pair_coeffs, rdm, b_tensor, gen_coeffs, act_coeffs):
    highest = lax.Precision.HIGHEST
    fitted = lax.dot_general(pair_coeffs, rdm, (((1,), (1,)), ((), ())), precision=highest, preferred_element_type=jnp.float32)
    fitted_blocks = fitted.reshape(N_AUX, AUX_DEV, NACT, NACT)
    slice_blocks = b_tensor.reshape(N_AUX, AUX_DEV, NACT, NORB)

    def accumulate(total, pieces):
        fit_block, slice_block = pieces
        return (total + jnp.einsum('qtu,qup->tp', fit_block, slice_block, precision=highest), None)
    fock, unused = lax.scan(accumulate, jnp.zeros((NACT, NORB), jnp.float32), (fitted_blocks, slice_blocks))
    grad = 2.0 * fock
    gnorm = jnp.sqrt(jnp.sum(grad * grad) + 1e-06)
    kappa = -NACT ** 0.5 * grad / gnorm
    direction = (NACT * NORB) ** 0.5 * grad / gnorm
    active_shift = jnp.dot(gen_coeffs, kappa.T, precision=highest, preferred_element_type=jnp.float32)
    general_shift = -jnp.dot(act_coeffs, kappa, precision=highest, preferred_element_type=jnp.float32)
    return (direction, active_shift, general_shift)
```

```python
import math

import jax
import jax.numpy as jnp
from jax import lax
from jax.sharding import Mesh, PartitionSpec as P

NY, NZ, NX = 4, 8, 4
X = ("xh", "xl")
HIGH = lax.Precision.HIGH
HIGHEST = lax.Precision.HIGHEST


def shift(value, axis, size, step):
    return lax.ppermute(value, axis, [(i, (i + step) % size) for i in range(size)])


def swap_core(value):
    return lax.ppermute(value, "co", [(0, 1), (1, 0)])


def ring_gather(block, axis, size, cut):
    found = {0: block}
    for k in range(1, size // 2):
        found[k] = shift(found[k - 1], axis, size, -1)
        found[size - k] = shift(found[(size - k + 1) % size], axis, size, 1)
    half = size // 2
    lower = shift(found[half - 1][:cut], axis, size, -1)
    upper = shift(found[half + 1][cut:], axis, size, 1)
    found[half] = jnp.concatenate([lower, upper], axis=0)
    return [found[k] for k in range(size)]


def on_device(pair_coeffs, rdm, b_tensor, gen_coeffs, act_coeffs):
    f32 = jnp.float32
    naux, nact, norb = b_tensor.shape
    rows_tu = rdm.shape[0]
    nt = rows_tu // nact
    half = naux // 2
    core = lax.axis_index("co")
    y = lax.axis_index("y")
    z = lax.axis_index("z")
    x = lax.axis_index("xh") * 2 + lax.axis_index("xl")

    first, second = pair_coeffs[:half], pair_coeffs[half:]
    mine = jnp.where(core == 0, first, second)
    other = jnp.where(core == 0, second, first)
    own_block = jnp.concatenate([mine, other], axis=0)

    pieces_p = ring_gather(own_block, "z", NZ, half)
    pieces_r = ring_gather(rdm, "y", NY, rows_tu // 2)
    gathered = jnp.concatenate(pieces_p, axis=0)
    parts = []
    for piece in pieces_r:
        parts.append(
            lax.dot_general(
                gathered, piece, (((1,), (1,)), ((), ())), precision=HIGH, preferred_element_type=f32
            ).reshape(NZ, 2, half, rows_tu)
        )
    part = jnp.stack(parts)
    kept = part[:, :, 0] + swap_core(part[:, :, 1])

    total = lax.dynamic_index_in_dim(kept, x, 0, keepdims=False)
    for s in range(1, NX):
        total = total + shift(lax.dynamic_index_in_dim(kept, (x + s) % NX, 0, keepdims=False), X, NX, s)

    mine_z = [total[0]] + [shift(total[k], "z", NZ, k) for k in range(1, NZ)]
    mine_z = jnp.stack(mine_z)
    mine_x = jnp.stack([mine_z] + [shift(mine_z, X, NX, s) for s in range(1, NX)])
    theirs = swap_core(mine_x)
    low = jnp.where(core == 0, mine_x, theirs)
    high = jnp.where(core == 0, theirs, mine_x)
    fitted = jnp.concatenate([low, high], axis=2).reshape(NX, NZ, naux, nt, nact)
    fock_part = jnp.einsum("skqtu,qup->sktp", fitted, b_tensor, precision=HIGH)
    fock_part = fock_part.reshape(nact, norb)

    s_of = (y + x - jnp.arange(NY)) % NY
    source = (
        s_of[None, :, None] * (NZ * nt) + jnp.arange(NZ)[:, None, None] * nt + jnp.arange(nt)[None, None, :]
    ).reshape(-1)
    order = (source[:, None] == jnp.arange(nact)[None, :]).astype(f32)
    fock_part = jnp.dot(order, fock_part, precision=HIGHEST, preferred_element_type=f32)
    fock_part = fock_part.reshape(NZ, NY * nt, norb)
    piece = fock_part[0]
    for k in range(1, NZ):
        piece = piece + shift(fock_part[k], "z", NZ, -k)
    full = piece
    for s in range(1, NY):
        full = full + shift(piece, "y", NY, s)
    everyone = jnp.stack([full] + [shift(full, "z", NZ, -k) for k in range(1, NZ)]).reshape(nact, norb)
    k_of = (jnp.arange(NZ) - z) % NZ
    source = (
        k_of[None, :, None] * (NY * nt) + jnp.arange(NY)[:, None, None] * nt + jnp.arange(nt)[None, None, :]
    ).reshape(-1)
    order = (source[:, None] == jnp.arange(nact)[None, :]).astype(f32)
    fock = jnp.dot(order, everyone, precision=HIGHEST, preferred_element_type=f32)

    grad = 2.0 * fock
    squares = jnp.sum(grad * grad)
    active_part = lax.dot_general(
        gen_coeffs, grad, (((1,), (1,)), ((), ())), precision=HIGH, preferred_element_type=f32
    )
    packed = jnp.concatenate([active_part, jnp.full((1, nact), squares, f32)], axis=0)
    packed = packed + swap_core(packed)
    summed = packed
    for s in range(1, NX):
        summed = summed + shift(packed, X, NX, s)
    general_raw = jnp.dot(act_coeffs, grad, precision=HIGH, preferred_element_type=f32)
    inverse = 1.0 / jnp.sqrt(summed[-1, 0] + 1e-06)
    step_scale = math.sqrt(nact)
    active_shift = (-step_scale * inverse) * summed[:-1]
    general_shift = (step_scale * inverse) * general_raw
    direction = (math.sqrt(nact * norb * 8) * inverse) * grad
    return (direction, active_shift, general_shift)


def solution(mesh):
    grid = Mesh(mesh.devices.reshape(NY, NZ, 2, 2, 2), ("y", "z", "xh", "co", "xl"))
    aux, cols = ("y", "z"), ("xh", "co", "xl")
    return jax.shard_map(
        on_device,
        mesh=grid,
        in_specs=(P(aux, cols), P(aux, cols), P(aux, None, cols), P(aux, cols), P(aux, None)),
        out_specs=(P(None, cols), P(aux, None), P(aux, cols)),
        check_vma=False,
    )
```

```python
import math

import jax
import jax.numpy as jnp
from jax import lax
from jax.sharding import Mesh, PartitionSpec as P

NY, NZ, NX = 4, 8, 4
X = ("xh", "xl")
HIGH = lax.Precision.HIGH
HIGHEST = lax.Precision.HIGHEST


def shift(value, axis, size, step):
    return lax.ppermute(value, axis, [(i, (i + step) % size) for i in range(size)])


def swap_core(value):
    return lax.ppermute(value, "co", [(0, 1), (1, 0)])


def ring_gather(block, axis, size, cut):
    found = {0: block}
    for k in range(1, size // 2):
        found[k] = shift(found[k - 1], axis, size, -1)
        found[size - k] = shift(found[(size - k + 1) % size], axis, size, 1)
    half = size // 2
    lower = shift(found[half - 1][:cut], axis, size, -1)
    upper = shift(found[half + 1][cut:], axis, size, 1)
    found[half] = jnp.concatenate([lower, upper], axis=0)
    return [found[k] for k in range(size)]


def on_device(pair_coeffs, rdm, b_tensor, gen_coeffs, act_coeffs):
    f32 = jnp.float32
    naux, nact, norb = b_tensor.shape
    rows_tu = rdm.shape[0]
    nt = rows_tu // nact
    half = naux // 2
    core = lax.axis_index("co")
    y = lax.axis_index("y")
    z = lax.axis_index("z")
    x = lax.axis_index("xh") * 2 + lax.axis_index("xl")

    pieces_r = ring_gather(rdm, "y", NY, rows_tu // 2)
    pieces_p = ring_gather(pair_coeffs, "z", NZ, half)
    gathered = jnp.concatenate(pieces_p, axis=0)
    parts = []
    for piece in pieces_r:
        parts.append(
            lax.dot_general(
                gathered, piece, (((1,), (1,)), ((), ())), precision=HIGH, preferred_element_type=f32
            ).reshape(2, NX, naux, rows_tu)
        )
    part = jnp.stack(parts, axis=2)
    lower, upper = part[0], part[1]
    kept = jnp.where(core == 0, lower, upper) + swap_core(jnp.where(core == 0, upper, lower))

    def block(s):
        return lax.dynamic_index_in_dim(kept, (x + s) % NX, 0, keepdims=False)

    far = block(2)
    up = shift(far[:, :half], X, NX, 1)
    down = shift(far[:, half:], X, NX, -1)
    after, before = block(1), block(3)
    after = jnp.concatenate([after[:, :half] + up, after[:, half:]], axis=1)
    before = jnp.concatenate([before[:, :half], before[:, half:] + down], axis=1)
    total = block(0) + shift(after, X, NX, 1) + shift(before, X, NX, -1)

    def rank(zz, xx, cc):
        return ((zz * 2 + xx // 2) * 2 + cc) * 2 + xx % 2

    pairs = [
        (rank(zz, xx, cc), rank((zz + xx + NX * cc) % NZ, xx, cc))
        for zz in range(NZ)
        for xx in range(NX)
        for cc in range(2)
    ]
    returned = lax.ppermute(total, ("z", "xh", "co", "xl"), pairs)

    after = shift(returned, X, NX, -1)
    before = shift(returned, X, NX, 1)
    far_low = shift(after[:, :half], X, NX, -1)
    far_high = shift(before[:, half:], X, NX, 1)
    far = jnp.concatenate([far_low, far_high], axis=1)
    mine_x = jnp.stack([returned, after, far, before])
    theirs = swap_core(mine_x)
    fitted = jnp.stack([mine_x, theirs]).reshape(2, NX, NY, naux, nt, nact)
    fock_part = jnp.einsum("csdqtu,qup->csdtp", fitted, b_tensor, precision=HIGH)
    fock_part = fock_part.reshape(nact, norb)

    y_of = jnp.arange(NY)[:, None]
    z_of = jnp.arange(NZ)[None, :]
    offset = (z - z_of - NX * core) % NZ
    dy = (y_of - y) % NY
    s = (offset % NX - x) % NX
    base = ((offset // NX * NX + s) * NY + dy) * nt
    source = (base[:, :, None] + jnp.arange(nt)).reshape(-1)
    order = (source[:, None] == jnp.arange(nact)[None, :]).astype(f32)
    fock_part = jnp.dot(order, fock_part, precision=HIGHEST, preferred_element_type=f32)
    spread = lax.all_to_all(
        fock_part.reshape(NY * NZ, nt, norb), ("y", "z"), split_axis=0, concat_axis=0, tiled=True
    )
    rows = jnp.sum(spread, axis=0, keepdims=True)
    fock = lax.all_to_all(
        jnp.broadcast_to(rows, spread.shape), ("y", "z"), split_axis=0, concat_axis=0, tiled=True
    ).reshape(nact, norb)

    grad = 2.0 * fock
    squares = jnp.sum(grad * grad)
    active_part = lax.dot_general(
        gen_coeffs, grad, (((1,), (1,)), ((), ())), precision=HIGH, preferred_element_type=f32
    )
    packed = jnp.concatenate([active_part, jnp.full((1, nact), squares, f32)], axis=0)
    packed = packed + swap_core(packed)
    summed = packed
    for s in range(1, NX):
        summed = summed + shift(packed, X, NX, s)
    general_raw = jnp.dot(act_coeffs, grad, precision=HIGH, preferred_element_type=f32)
    inverse = 1.0 / jnp.sqrt(summed[-1, 0] + 1e-06)
    step_scale = math.sqrt(nact)
    active_shift = (-step_scale * inverse) * summed[:-1]
    general_shift = (step_scale * inverse) * general_raw
    direction = (math.sqrt(nact * norb * 8) * inverse) * grad
    return (direction, active_shift, general_shift)


def solution(mesh):
    grid = Mesh(mesh.devices.reshape(NY, NZ, 2, 2, 2), ("y", "z", "xh", "co", "xl"))
    aux, cols = ("y", "z"), ("xh", "co", "xl")
    return jax.shard_map(
        on_device,
        mesh=grid,
        in_specs=(P(aux, cols), P(aux, cols), P(aux, None, cols), P(aux, cols), P(aux, None)),
        out_specs=(P(None, cols), P(aux, None), P(aux, cols)),
        check_vma=False,
    )
```

```python
import functools
import math

import jax
import jax.numpy as jnp
from jax import lax
from jax.experimental import pallas as pl
from jax.experimental.pallas import tpu as pltpu
from jax.sharding import Mesh, PartitionSpec as P

NY, NZ, NX = 4, 8, 4
X = ("xh", "xl")
HIGH = lax.Precision.HIGH
HIGHEST = lax.Precision.HIGHEST


def shift(value, axis, size, step):
    return lax.ppermute(value, axis, [(i, (i + step) % size) for i in range(size)])


def swap_core(value):
    return lax.ppermute(value, "co", [(0, 1), (1, 0)])


def ring_gather(block, axis, size, tie):
    found = {0: block}
    half = size // 2
    for k in range(1, half):
        found[k] = shift(found[k - 1], axis, size, -1)
        found[size - k] = shift(found[(size - k + 1) % size], axis, size, 1)
    found[half] = shift(found[half - 1] + tie, axis, size, -1)
    return [found[k] for k in range(size)]


def split(value):
    head = value.astype(jnp.bfloat16)
    return head, (value - head.astype(jnp.float32)).astype(jnp.bfloat16)


def position():
    return lax.axis_index("y"), lax.axis_index("z"), lax.axis_index("xh") * 2 + lax.axis_index("xl"), lax.axis_index("co")


def product(left, right, dims):
    head, rest = left
    first, second = right
    total = lax.dot_general(head, first, dims, preferred_element_type=jnp.float32)
    total += lax.dot_general(head, second, dims, preferred_element_type=jnp.float32)
    return total + lax.dot_general(rest, first, dims, preferred_element_type=jnp.float32)


def pair_kernel(n_p, *refs):
    p_refs, r_refs = refs[:n_p], refs[n_p:-6]
    kept_ref, sent_ref, p_head, p_rest, r_head, r_rest = refs[-6:]
    _, _, x, core = position()
    half = kept_ref.shape[0]
    for k, ref in enumerate(p_refs):
        rows = ref.shape[0]
        start = ((k // NX) ^ core) * half + ((k % NX - x) & (NX - 1)) * rows
        place = pl.ds(pl.multiple_of(start, 16), rows)
        p_head[place, :], p_rest[place, :] = split(ref[...])
    start = 0
    for ref in r_refs:
        rows = ref.shape[0]
        r_head[start : start + rows, :], r_rest[start : start + rows, :] = split(ref[...])
        start += rows
    for low in range(0, start, 256):
        high = min(low + 256, start)
        pieces = (r_head[low:high, :], r_rest[low:high, :])
        total = product((p_head[...], p_rest[...]), pieces, (((1,), (1,)), ((), ())))
        kept_ref[:, low:high] = total[:half]
        sent_ref[:, low:high] = total[half:]


def pair_product(p_pieces, r_pieces):
    depth = p_pieces[0].shape[1]
    n_rows = sum(p.shape[0] for p in p_pieces)
    n_cols = sum(r.shape[0] for r in r_pieces)
    vmem = pl.BlockSpec(memory_space=pltpu.VMEM)
    shape = jax.ShapeDtypeStruct((n_rows // 2, n_cols), jnp.float32)
    return pl.pallas_call(
        functools.partial(pair_kernel, len(p_pieces)),
        out_shape=(shape, shape),
        in_specs=[vmem] * (len(p_pieces) + len(r_pieces)),
        out_specs=(vmem, vmem),
        scratch_shapes=[pltpu.VMEM((n, depth), jnp.bfloat16) for n in (n_rows, n_rows, n_cols, n_cols)],
        compiler_params=pltpu.CompilerParams(vmem_limit_bytes=20 * 2**20),
        cost_estimate=pl.CostEstimate(flops=1000, bytes_accessed=1000, transcendentals=0),
    )(*p_pieces, *r_pieces)


def join_kernel(*refs):
    chunks, (own_ref, after_ref, before_ref, low_ref, high_ref) = refs[:-5], refs[-5:]
    rows = own_ref.shape[0]
    start = 0
    for kept_ref, got_ref in zip(chunks[::2], chunks[1::2]):
        lanes = slice(start, start + kept_ref.shape[1])
        start = lanes.stop
        total = kept_ref[...] + got_ref[...]
        own_ref[:, lanes] = total[:rows]
        after_ref[:, lanes] = total[rows : 2 * rows]
        low_ref[:, lanes] = total[2 * rows : 2 * rows + rows // 2]
        high_ref[:, lanes] = total[2 * rows + rows // 2 : 3 * rows]
        before_ref[:, lanes] = total[3 * rows :]


def add_kernel(after_ref, up_ref, before_ref, down_ref, after_out, before_out):
    half = up_ref.shape[0]
    after_out[:half] = after_ref[:half] + up_ref[...]
    after_out[half:] = after_ref[half:]
    before_out[:half] = before_ref[:half]
    before_out[half:] = before_ref[half:] + down_ref[...]


def sum_over_x(chunks):
    rows = chunks[0].shape[0] // NX
    lanes = sum(chunk.shape[1] for chunk in chunks[::2])
    whole, part = (jax.ShapeDtypeStruct((n, lanes), jnp.float32) for n in (rows, rows // 2))
    small = pltpu.CompilerParams(vmem_limit_bytes=8 * 2**20)
    own, after, before, low, high = pl.pallas_call(
        join_kernel, out_shape=(whole, whole, whole, part, part), compiler_params=small
    )(*chunks)
    up, down = shift(low, X, NX, 1), shift(high, X, NX, -1)
    after, before = pl.pallas_call(add_kernel, out_shape=(whole, whole), compiler_params=small)(after, up, before, down)
    return own + shift(after, X, NX, 1) + shift(before, X, NX, -1)


def fock_kernel(sizes, nact, per_step, *refs):
    b_ref, out_ref, sorted_ref, acc_ref = refs[-4:]
    y, z, x, core = position()
    naux = b_ref.shape[0]
    steps = naux // per_step

    n_t = refs[0].shape[1] // nact // NY
    at = 0
    for g, size in enumerate(sizes):
        c, s = g // NX, g % NX
        zb = (z - ((x + s) & (NX - 1)) - NX * ((core + c) & 1)) & (NZ - 1)
        base = 0
        for ref in refs[at : at + size]:
            rows = ref.shape[0]
            for j, dy in enumerate((0, 1, 3, 2)):
                first = (((y + dy) & (NY - 1)) * NZ + zb) * n_t
                for t in range(n_t):
                    place = pl.ds(pl.multiple_of((first + t) * naux + base, 8), rows)
                    low = (j * n_t + t) * nact
                    sorted_ref[place, :] = ref[:, low : low + nact]
            base += rows
        at += size
    acc_ref[...] = jnp.zeros_like(acc_ref)

    def step(i, carry):
        total = acc_ref[...]
        for j in range(per_step):
            q = i * per_step + j
            head, rest = split(sorted_ref[pl.ds(q, nact, stride=naux), :])
            b_head, b_rest = split(b_ref[q])
            both = jnp.dot(jnp.concatenate([head, rest]), b_head, preferred_element_type=jnp.float32)
            total += jnp.dot(head, b_rest, preferred_element_type=jnp.float32) + both[:nact] + both[nact:]
        acc_ref[...] = total
        return carry

    lax.fori_loop(0, steps, step, 0)
    half, lanes = out_ref.shape[1:]
    norb = acc_ref.shape[1]
    for h in range(2):
        for j in range(NX):
            wide = min(lanes, norb - j * lanes)
            if wide < lanes:
                out_ref[h * NX + j] = jnp.zeros((half, lanes), jnp.float32)
            out_ref[h * NX + j, :, :wide] = acc_ref[h * half : (h + 1) * half, j * lanes : j * lanes + wide]


def fock_product(fitted, b_tensor, lanes):
    naux, nact, norb = b_tensor.shape
    per_step = 8
    flat = [piece for group in fitted for piece in group]
    vmem = pl.BlockSpec(memory_space=pltpu.VMEM)
    return pl.pallas_call(
        functools.partial(fock_kernel, [len(group) for group in fitted], nact, per_step),
        out_shape=jax.ShapeDtypeStruct((2 * NX, nact // 2, lanes), jnp.float32),
        in_specs=[vmem] * (len(flat) + 1),
        out_specs=vmem,
        scratch_shapes=[
            pltpu.VMEM((nact * naux, nact), jnp.float32),
            pltpu.VMEM((nact, norb), jnp.float32),
        ],
        compiler_params=pltpu.CompilerParams(vmem_limit_bytes=16 * 2**20),
    )(*flat, b_tensor)


def grad_kernel(tiles_ref, gen_ref, grad_ref, packed_ref):
    half, lanes = tiles_ref.shape[1:]
    nact, norb = grad_ref.shape
    for h in range(2):
        for j in range(NX):
            wide = min(lanes, norb - j * lanes)
            grad_ref[h * half : (h + 1) * half, j * lanes : j * lanes + wide] = 2.0 * tiles_ref[h * NX + j, :, :wide]
    grad = grad_ref[...]
    packed_ref[:nact, :] = product(split(grad), split(gen_ref[...]), (((1,), (0,)), ((), ())))
    rows, cols = packed_ref.shape
    packed_ref[nact:, :] = jnp.zeros((rows - nact, cols), jnp.float32) + jnp.sum(grad * grad)


def general_kernel(grad_ref, act_ref, out_ref):
    out_ref[...] = product(split(grad_ref[...].T), split(act_ref[...]), (((1,), (0,)), ((), ())))


def scale_kernel(step_scale, whole_scale, a_ref, b_ref, c_ref, d_ref, grad_ref, raw_ref, dir_ref, act_ref, gen_ref):
    total = (a_ref[...] + c_ref[...]) + (b_ref[...] + d_ref[...])
    nact = act_ref.shape[0]
    inverse = 1.0 / jnp.sqrt(total[nact : nact + 1, 0:1] + 1e-06)
    dir_ref[...] = (whole_scale * inverse) * grad_ref[...]
    act_ref[...] = (-step_scale * inverse) * total[:nact]
    gen_ref[...] = (step_scale * inverse) * raw_ref[...]


def tail(tiles, gen_coeffs, act_coeffs, norb):
    nact = act_coeffs.shape[1]
    nbas = gen_coeffs.shape[0]
    f32 = jnp.float32
    shape = jax.ShapeDtypeStruct
    small = pltpu.CompilerParams(vmem_limit_bytes=8 * 2**20)
    grad, packed = pl.pallas_call(
        grad_kernel, out_shape=(shape((nact, norb), f32), shape((nact + 8, nbas), f32)), compiler_params=small
    )(tiles, gen_coeffs.T)
    raw = pl.pallas_call(general_kernel, out_shape=shape((norb, nbas), f32), compiler_params=small)(grad, act_coeffs.T)
    packed = packed + swap_core(packed)
    others = [shift(packed, X, NX, s) for s in range(1, NX)]
    direction, active, general = pl.pallas_call(
        functools.partial(scale_kernel, math.sqrt(nact), math.sqrt(nact * norb * 2 * NX)),
        out_shape=(shape((nact, norb), f32), shape((nact, nbas), f32), shape((norb, nbas), f32)),
        compiler_params=small,
    )(packed, *others, grad, raw)
    return direction, active.T, general.T


def on_device(pair_coeffs, rdm, b_tensor, gen_coeffs, act_coeffs):
    naux, nact, norb = b_tensor.shape
    rows_tu = rdm.shape[0]
    nt = rows_tu // nact
    half = naux // 2
    ahead, behind = shift(rdm, "y", NY, -1), shift(rdm, "y", NY, 1)
    cut = rows_tu // 2
    lower, upper = ahead[:cut], behind[cut:]
    gathered = ring_gather(pair_coeffs, "z", NZ, 0.0 * (lower[0, 0] + upper[0, 0]))
    across = [shift(lower, "y", NY, -1), shift(upper, "y", NY, 1)]

    chunks = []
    for pieces in ([rdm, ahead, behind], across):
        kept, sent = pair_product(gathered, pieces)
        chunks += [kept, swap_core(sent)]
    total = sum_over_x(chunks)

    def rank(zz, xx, cc):
        return ((zz * 2 + xx // 2) * 2 + cc) * 2 + xx % 2

    pairs = [
        (rank(zz, xx, cc), rank((zz + xx + NX * cc) % NZ, xx, cc))
        for zz in range(NZ)
        for xx in range(NX)
        for cc in range(2)
    ]
    returned = lax.ppermute(total, ("z", "xh", "co", "xl"), pairs)

    after = shift(returned, X, NX, -1)
    before = shift(returned, X, NX, 1)
    far_low = shift(after[:half], X, NX, -1)
    far_high = shift(before[half:], X, NX, 1)
    mine = [[returned], [after], [far_low, far_high], [before]]
    theirs = [[swap_core(piece) for piece in group] for group in mine]

    lanes = 128 if norb > 128 else norb // NX
    tiles = fock_product(mine + theirs, b_tensor, lanes)
    piece = jnp.sum(lax.all_to_all(tiles, "z", split_axis=0, concat_axis=0, tiled=True), axis=0)
    piece = (piece + shift(piece, "y", NY, 2)) + (shift(piece, "y", NY, 1) + shift(piece, "y", NY, -1))
    tiles = lax.all_to_all(
        jnp.broadcast_to(piece[None], tiles.shape), "z", split_axis=0, concat_axis=0, tiled=True
    )
    return tail(tiles, gen_coeffs, act_coeffs, norb)


def solution(mesh):
    grid = Mesh(mesh.devices.reshape(NY, NZ, 2, 2, 2), ("y", "z", "xh", "co", "xl"))
    aux, cols = ("y", "z"), ("xh", "co", "xl")
    return jax.shard_map(
        on_device,
        mesh=grid,
        in_specs=(P(aux, cols), P(aux, cols), P(aux, None, cols), P(aux, cols), P(aux, None)),
        out_specs=(P(None, cols), P(aux, None), P(aux, cols)),
        check_vma=False,
    )
```

```python
import functools
import math

import jax
import jax.numpy as jnp
from jax import lax
from jax.experimental import pallas as pl
from jax.experimental.pallas import tpu as pltpu
from jax.sharding import Mesh, PartitionSpec as P

NY, NZ, NX = 4, 8, 4
TURN = 2
X = ("xh", "xl")
SMALL = pltpu.CompilerParams(vmem_limit_bytes=8 * 2**20)


def shift(value, axis, size, step):
    return lax.ppermute(value, axis, [(i, (i + step) % size) for i in range(size)])


def swap_core(value):
    return lax.ppermute(value, "co", [(0, 1), (1, 0)])


def swap(value, axis, size, mask):
    return lax.ppermute(value, axis, [(i, i ^ mask) for i in range(size)])


def split(value):
    head = value.astype(jnp.bfloat16)
    return head, (value - head.astype(jnp.float32)).astype(jnp.bfloat16)


def position():
    return lax.axis_index("y"), lax.axis_index("z"), lax.axis_index("xh") * 2 + lax.axis_index("xl"), lax.axis_index("co")


def product(left, right, dims):
    head, rest = left
    first, second = right
    total = lax.dot_general(head, first, dims, preferred_element_type=jnp.float32)
    total += lax.dot_general(head, second, dims, preferred_element_type=jnp.float32)
    return total + lax.dot_general(rest, first, dims, preferred_element_type=jnp.float32)


def pair_kernel(n_p, fresh, *refs):
    p_head, p_rest = refs[-2:]
    p_refs = refs[:n_p]
    if fresh:
        r_refs, (kept_ref, sent_ref, r_head, r_rest) = refs[n_p:-6], refs[-6:-2]
        start = 0
        for ref in r_refs:
            rows = ref.shape[0]
            r_head[start : start + rows, :], r_rest[start : start + rows, :] = split(ref[...])
            start += rows
    else:
        r_head, r_rest, kept_ref, sent_ref = refs[n_p:-2]
    _, _, x, core = position()
    half, n_cols = kept_ref.shape
    for k, ref in enumerate(p_refs):
        rows = ref.shape[0]
        start = ((k // NX) ^ core) * half + ((k % NX - x) & (NX - 1)) * rows
        place = pl.ds(pl.multiple_of(start, 16), rows)
        p_head[place, :], p_rest[place, :] = split(ref[...])
    for low in range(0, n_cols, 256):
        high = min(low + 256, n_cols)
        pieces = (r_head[low:high, :], r_rest[low:high, :])
        total = product((p_head[...], p_rest[...]), pieces, (((1,), (1,)), ((), ())))
        kept_ref[:, low:high] = total[:half]
        sent_ref[:, low:high] = total[half:]


def pair_product(p_pieces, rows, fresh):
    depth = p_pieces[0].shape[1]
    n_rows = sum(p.shape[0] for p in p_pieces)
    n_cols = sum(r.shape[0] for r in rows) if fresh else rows[0].shape[0]
    shape = jax.ShapeDtypeStruct((n_rows // 2, n_cols), jnp.float32)
    parts = jax.ShapeDtypeStruct((n_cols, depth), jnp.bfloat16)
    return pl.pallas_call(
        functools.partial(pair_kernel, len(p_pieces), fresh),
        out_shape=(shape, shape) + ((parts, parts) if fresh else ()),
        scratch_shapes=[pltpu.VMEM((n_rows, depth), jnp.bfloat16)] * 2,
        compiler_params=pltpu.CompilerParams(vmem_limit_bytes=16 * 2**20),
        cost_estimate=pl.CostEstimate(flops=1000, bytes_accessed=1000, transcendentals=0),
    )(*p_pieces, *rows)


def join_kernel(*refs):
    chunks, (own_ref, after_ref, before_ref, low_ref, high_ref) = refs[:-5], refs[-5:]
    rows = own_ref.shape[0]
    start = 0
    for kept_ref, got_ref in zip(chunks[::2], chunks[1::2]):
        lanes = slice(start, start + kept_ref.shape[1])
        start = lanes.stop
        total = kept_ref[...] + got_ref[...]
        own_ref[:, lanes] = total[:rows]
        after_ref[:, lanes] = total[rows : 2 * rows]
        low_ref[:, lanes] = total[2 * rows : 2 * rows + rows // 2]
        high_ref[:, lanes] = total[2 * rows + rows // 2 : 3 * rows]
        before_ref[:, lanes] = total[3 * rows :]


def add_kernel(after_ref, up_ref, before_ref, down_ref, after_out, before_out):
    half = up_ref.shape[0]
    after_out[:half] = after_ref[:half] + up_ref[...]
    after_out[half:] = after_ref[half:]
    before_out[:half] = before_ref[:half]
    before_out[half:] = before_ref[half:] + down_ref[...]


def sides_kernel(own_ref, one_ref, two_ref, first_ref, second_ref):
    total = own_ref[...] + one_ref[...] + two_ref[...]
    lanes = first_ref.shape[1]
    first_ref[...] = total[:, :lanes]
    second_ref[...] = total[:, lanes:]


def lanes_kernel(first_ref, second_ref, out_ref):
    lanes = first_ref.shape[1]
    out_ref[:, :lanes] = first_ref[...]
    out_ref[:, lanes:] = second_ref[...]


def sum_over_x(chunks):
    rows = chunks[0].shape[0] // NX
    lanes = sum(chunk.shape[1] for chunk in chunks[::2])
    whole, part = (jax.ShapeDtypeStruct((n, lanes), jnp.float32) for n in (rows, rows // 2))
    own, after, before, low, high = pl.pallas_call(
        join_kernel, out_shape=(whole, whole, whole, part, part), compiler_params=SMALL
    )(*chunks)
    up, down = shift(low, X, NX, 1), shift(high, X, NX, -1)
    after, before = pl.pallas_call(add_kernel, out_shape=(whole, whole), compiler_params=SMALL)(after, up, before, down)
    side = jax.ShapeDtypeStruct((rows, lanes // 2), jnp.float32)
    return pl.pallas_call(sides_kernel, out_shape=(side, side), compiler_params=SMALL)(
        own, shift(after, X, NX, 1), shift(before, X, NX, -1)
    )


def fock_kernel(sizes, nact, per_step, *refs):
    b_ref, out_ref, sorted_ref, acc_ref = refs[-4:]
    y, z, x, core = position()
    naux = b_ref.shape[0]
    steps = naux // per_step

    n_t = refs[0].shape[1] // nact // NY
    at = 0
    for g, size in enumerate(sizes):
        c, s = g // NX, g % NX
        zb = (z - ((x + s) & (NX - 1)) - NX * ((core + c) & 1)) & (NZ - 1)
        base = 0
        for ref in refs[at : at + size]:
            rows = ref.shape[0]
            for j, mask in enumerate((0, 1, 3, 2)):
                turned = zb if j < 2 else (zb - TURN) & (NZ - 1)
                first = ((y ^ mask) * NZ + turned) * n_t
                for t in range(n_t):
                    place = pl.ds(pl.multiple_of((first + t) * naux + base, 8), rows)
                    low = (j * n_t + t) * nact
                    sorted_ref[place, :] = ref[:, low : low + nact]
            base += rows
        at += size
    acc_ref[...] = jnp.zeros_like(acc_ref)

    def step(i, carry):
        total = acc_ref[...]
        for j in range(per_step):
            q = i * per_step + j
            head, rest = split(sorted_ref[pl.ds(q, nact, stride=naux), :])
            b_head, b_rest = split(b_ref[q])
            both = jnp.dot(jnp.concatenate([head, rest]), b_head, preferred_element_type=jnp.float32)
            total += jnp.dot(head, b_rest, preferred_element_type=jnp.float32) + both[:nact] + both[nact:]
        acc_ref[...] = total
        return carry

    lax.fori_loop(0, steps, step, 0)
    half, lanes = out_ref.shape[1:]
    norb = acc_ref.shape[1]
    for h in range(2):
        for j in range(NX):
            wide = min(lanes, norb - j * lanes)
            if wide < lanes:
                out_ref[h * NX + j] = jnp.zeros((half, lanes), jnp.float32)
            out_ref[h * NX + j, :, :wide] = acc_ref[h * half : (h + 1) * half, j * lanes : j * lanes + wide]


def fock_product(fitted, b_tensor, lanes):
    naux, nact, norb = b_tensor.shape
    per_step = 8
    flat = [piece for group in fitted for piece in group]
    vmem = pl.BlockSpec(memory_space=pltpu.VMEM)
    return pl.pallas_call(
        functools.partial(fock_kernel, [len(group) for group in fitted], nact, per_step),
        out_shape=jax.ShapeDtypeStruct((2 * NX, nact // 2, lanes), jnp.float32),
        in_specs=[vmem] * (len(flat) + 1),
        out_specs=vmem,
        scratch_shapes=[
            pltpu.VMEM((nact * naux, nact), jnp.float32),
            pltpu.VMEM((nact, norb), jnp.float32),
        ],
        compiler_params=pltpu.CompilerParams(vmem_limit_bytes=16 * 2**20),
    )(*flat, b_tensor)


def grad_kernel(tiles_ref, gen_ref, grad_ref, packed_ref):
    half, lanes = tiles_ref.shape[1:]
    nact, norb = grad_ref.shape
    for h in range(2):
        for j in range(NX):
            wide = min(lanes, norb - j * lanes)
            grad_ref[h * half : (h + 1) * half, j * lanes : j * lanes + wide] = 2.0 * tiles_ref[h * NX + j, :, :wide]
    grad = grad_ref[...]
    packed_ref[:nact, :] = product(split(grad), split(gen_ref[...]), (((1,), (0,)), ((), ())))
    rows, cols = packed_ref.shape
    packed_ref[nact:, :] = jnp.zeros((rows - nact, cols), jnp.float32) + jnp.sum(grad * grad)


def general_kernel(grad_ref, act_ref, out_ref):
    out_ref[...] = product(split(grad_ref[...].T), split(act_ref[...]), (((1,), (0,)), ((), ())))


def scale_kernel(step_scale, whole_scale, a_ref, b_ref, c_ref, d_ref, grad_ref, raw_ref, dir_ref, act_ref, gen_ref):
    total = (a_ref[...] + c_ref[...]) + (b_ref[...] + d_ref[...])
    nact = act_ref.shape[0]
    inverse = 1.0 / jnp.sqrt(total[nact : nact + 1, 0:1] + 1e-06)
    dir_ref[...] = (whole_scale * inverse) * grad_ref[...]
    act_ref[...] = (-step_scale * inverse) * total[:nact]
    gen_ref[...] = (step_scale * inverse) * raw_ref[...]


def tail(tiles, gen_coeffs, act_coeffs, norb):
    nact = act_coeffs.shape[1]
    nbas = gen_coeffs.shape[0]
    f32 = jnp.float32
    shape = jax.ShapeDtypeStruct
    grad, packed = pl.pallas_call(
        grad_kernel, out_shape=(shape((nact, norb), f32), shape((nact + 8, nbas), f32)), compiler_params=SMALL
    )(tiles, gen_coeffs.T)
    raw = pl.pallas_call(general_kernel, out_shape=shape((norb, nbas), f32), compiler_params=SMALL)(grad, act_coeffs.T)
    packed = packed + swap_core(packed)
    others = [swap(packed, X, NX, mask) for mask in (1, 2, 3)]
    direction, active, general = pl.pallas_call(
        functools.partial(scale_kernel, math.sqrt(nact), math.sqrt(nact * norb * 2 * NX)),
        out_shape=(shape((nact, norb), f32), shape((nact, nbas), f32), shape((norb, nbas), f32)),
        compiler_params=SMALL,
    )(packed, *others, grad, raw)
    return direction, active.T, general.T


def on_device(pair_coeffs, rdm, b_tensor, gen_coeffs, act_coeffs):
    naux, nact, norb = b_tensor.shape
    half = naux // 2
    rows = [rdm, swap(rdm, "y", NY, 1)]
    near = {0: pair_coeffs}
    far = {0: swap(pair_coeffs, "y", NY, 3)}
    for k in range(1, NZ // 2):
        for found in (near, far):
            if found is near or k < 3:
                found[k] = shift(found[k - 1], "z", NZ, -1)
                found[NZ - k] = shift(found[(NZ - k + 1) % NZ], "z", NZ, 1)
    near[4] = shift(near[3], "z", NZ, -1)
    for k in (3, 5, 4):
        far[k] = swap(near[k], "y", NY, 3)

    kept, sent, *rows = pair_product([near[k] for k in range(NZ)], rows, True)
    chunks = [kept, swap_core(sent)]
    kept, sent = pair_product([far[(k + TURN) % NZ] for k in range(NZ)], rows, False)
    chunks += [kept, swap_core(sent)]
    first, second = sum_over_x(chunks)

    def rank(yy, zz, xx, cc):
        return (((yy * NZ + zz % NZ) * 2 + xx // 2) * 2 + cc) * 2 + xx % 2

    def send_home(value, mask, turn):
        pairs = [
            (rank(yy, zz, xx, cc), rank(yy ^ mask, zz + xx + NX * cc + turn, xx, cc))
            for yy in range(NY)
            for zz in range(NZ)
            for xx in range(NX)
            for cc in range(2)
        ]
        return lax.ppermute(value, ("y", "z", "xh", "co", "xl"), pairs)

    returned = pl.pallas_call(
        lanes_kernel,
        out_shape=jax.ShapeDtypeStruct((naux, 2 * first.shape[1]), first.dtype),
        compiler_params=SMALL,
    )(send_home(first, 0, 0), send_home(second, 3, TURN))

    after = shift(returned, X, NX, -1)
    before = shift(returned, X, NX, 1)
    far_low = shift(after[:half], X, NX, -1)
    far_high = shift(before[half:], X, NX, 1)
    mine = [[returned], [after], [far_low, far_high], [before]]
    theirs = [[swap_core(piece) for piece in group] for group in mine]

    lanes = 128 if norb > 128 else norb // NX
    tiles = fock_product(mine + theirs, b_tensor, lanes)
    piece = jnp.sum(lax.all_to_all(tiles, "z", split_axis=0, concat_axis=0, tiled=True), axis=0)
    piece = (piece + swap(piece, "y", NY, 2)) + (swap(piece, "y", NY, 1) + swap(piece, "y", NY, 3))
    tiles = lax.all_to_all(
        jnp.broadcast_to(piece[None], tiles.shape), "z", split_axis=0, concat_axis=0, tiled=True
    )
    return tail(tiles, gen_coeffs, act_coeffs, norb)


def solution(mesh):
    grid = Mesh(mesh.devices.reshape(NY, NZ, 2, 2, 2), ("y", "z", "xh", "co", "xl"))
    aux, cols = ("y", "z"), ("xh", "co", "xl")
    return jax.shard_map(
        on_device,
        mesh=grid,
        in_specs=(P(aux, cols), P(aux, cols), P(aux, None, cols), P(aux, cols), P(aux, None)),
        out_specs=(P(None, cols), P(aux, None), P(aux, cols)),
        check_vma=False,
    )
```

```python
import functools
import math

import jax
import jax.numpy as jnp
from jax import lax
from jax.experimental import pallas as pl
from jax.experimental.pallas import tpu as pltpu
from jax.sharding import Mesh, PartitionSpec as P

NY, NZ, NX = 4, 8, 4
TURN = 2
X = ("xh", "xl")
SMALL = pltpu.CompilerParams(vmem_limit_bytes=8 * 2**20)


def shift(value, axis, size, step):
    return lax.ppermute(value, axis, [(i, (i + step) % size) for i in range(size)])


def swap_core(value):
    return lax.ppermute(value, "co", [(0, 1), (1, 0)])


def swap(value, axis, size, mask):
    return lax.ppermute(value, axis, [(i, i ^ mask) for i in range(size)])


def split(value):
    head = value.astype(jnp.bfloat16)
    return head, (value - head.astype(jnp.float32)).astype(jnp.bfloat16)


def position():
    return lax.axis_index("y"), lax.axis_index("z"), lax.axis_index("xh") * 2 + lax.axis_index("xl"), lax.axis_index("co")


def product(left, right, dims):
    head, rest = left
    first, second = right
    total = lax.dot_general(head, first, dims, preferred_element_type=jnp.float32)
    total += lax.dot_general(head, second, dims, preferred_element_type=jnp.float32)
    return total + lax.dot_general(rest, first, dims, preferred_element_type=jnp.float32)


def pair_kernel(n_p, fresh, *refs):
    p_head, p_rest = refs[-2:]
    p_refs = refs[:n_p]
    if fresh:
        r_refs, (kept_ref, sent_ref, r_head, r_rest) = refs[n_p:-6], refs[-6:-2]
        start = 0
        for ref in r_refs:
            rows = ref.shape[0]
            r_head[start : start + rows, :], r_rest[start : start + rows, :] = split(ref[...])
            start += rows
    else:
        r_head, r_rest, kept_ref, sent_ref = refs[n_p:-2]
    _, _, x, core = position()
    half, n_cols = kept_ref.shape
    for k, ref in enumerate(p_refs):
        rows = ref.shape[0]
        start = ((k // NX) ^ core) * half + ((k % NX - x) & (NX - 1)) * rows
        place = pl.ds(pl.multiple_of(start, 16), rows)
        p_head[place, :], p_rest[place, :] = split(ref[...])
    for low in range(0, n_cols, 256):
        high = min(low + 256, n_cols)
        pieces = (r_head[low:high, :], r_rest[low:high, :])
        total = product((p_head[...], p_rest[...]), pieces, (((1,), (1,)), ((), ())))
        kept_ref[:, low:high] = total[:half]
        sent_ref[:, low:high] = total[half:]


def pair_product(p_pieces, rows, fresh):
    depth = p_pieces[0].shape[1]
    n_rows = sum(p.shape[0] for p in p_pieces)
    n_cols = sum(r.shape[0] for r in rows) if fresh else rows[0].shape[0]
    shape = jax.ShapeDtypeStruct((n_rows // 2, n_cols), jnp.float32)
    parts = jax.ShapeDtypeStruct((n_cols, depth), jnp.bfloat16)
    return pl.pallas_call(
        functools.partial(pair_kernel, len(p_pieces), fresh),
        out_shape=(shape, shape) + ((parts, parts) if fresh else ()),
        scratch_shapes=[pltpu.VMEM((n_rows, depth), jnp.bfloat16)] * 2,
        compiler_params=pltpu.CompilerParams(vmem_limit_bytes=16 * 2**20),
        cost_estimate=pl.CostEstimate(flops=1000, bytes_accessed=1000, transcendentals=0),
    )(*p_pieces, *rows)


def join_kernel(*refs):
    chunks, (own_ref, after_ref, before_ref, low_ref, high_ref) = refs[:-5], refs[-5:]
    rows = own_ref.shape[0]
    start = 0
    for kept_ref, got_ref in zip(chunks[::2], chunks[1::2]):
        lanes = slice(start, start + kept_ref.shape[1])
        start = lanes.stop
        total = kept_ref[...] + got_ref[...]
        own_ref[:, lanes] = total[:rows]
        after_ref[:, lanes] = total[rows : 2 * rows]
        low_ref[:, lanes] = total[2 * rows : 2 * rows + rows // 2]
        high_ref[:, lanes] = total[2 * rows + rows // 2 : 3 * rows]
        before_ref[:, lanes] = total[3 * rows :]


def add_kernel(after_ref, up_ref, before_ref, down_ref, after_out, before_out):
    half = up_ref.shape[0]
    after_out[:half] = after_ref[:half] + up_ref[...]
    after_out[half:] = after_ref[half:]
    before_out[:half] = before_ref[:half]
    before_out[half:] = before_ref[half:] + down_ref[...]


def sides_kernel(own_ref, one_ref, two_ref, first_ref, second_ref):
    total = own_ref[...] + one_ref[...] + two_ref[...]
    lanes = first_ref.shape[1]
    first_ref[...] = total[:, :lanes]
    second_ref[...] = total[:, lanes:]


def lanes_kernel(first_ref, second_ref, out_ref):
    lanes = first_ref.shape[1]
    out_ref[:, :lanes] = first_ref[...]
    out_ref[:, lanes:] = second_ref[...]


def sum_over_x(chunks):
    rows = chunks[0].shape[0] // NX
    lanes = sum(chunk.shape[1] for chunk in chunks[::2])
    whole, part = (jax.ShapeDtypeStruct((n, lanes), jnp.float32) for n in (rows, rows // 2))
    own, after, before, low, high = pl.pallas_call(
        join_kernel, out_shape=(whole, whole, whole, part, part), compiler_params=SMALL
    )(*chunks)
    up, down = shift(low, X, NX, 1), shift(high, X, NX, -1)
    after, before = pl.pallas_call(add_kernel, out_shape=(whole, whole), compiler_params=SMALL)(after, up, before, down)
    side = jax.ShapeDtypeStruct((rows, lanes // 2), jnp.float32)
    return pl.pallas_call(sides_kernel, out_shape=(side, side), compiler_params=SMALL)(
        own, shift(after, X, NX, 1), shift(before, X, NX, -1)
    )


def fock_kernel(sizes, nact, per_step, *refs):
    b_ref, out_ref, sorted_ref, acc_ref = refs[-4:]
    y, z, x, core = position()
    naux = b_ref.shape[0]
    steps = naux // per_step

    n_t = refs[0].shape[1] // nact // NY
    at = 0
    for g, size in enumerate(sizes):
        c, s = g // NX, g % NX
        zb = (z - ((x + s) & (NX - 1)) - NX * ((core + c) & 1)) & (NZ - 1)
        base = 0
        for ref in refs[at : at + size]:
            rows = ref.shape[0]
            for j, mask in enumerate((0, 1, 3, 2)):
                turned = zb if j < 2 else (zb - TURN) & (NZ - 1)
                first = ((y ^ mask) * NZ + turned) * n_t
                for t in range(n_t):
                    place = pl.ds(pl.multiple_of((first + t) * naux + base, 8), rows)
                    low = (j * n_t + t) * nact
                    sorted_ref[place, :] = ref[:, low : low + nact]
            base += rows
        at += size
    acc_ref[...] = jnp.zeros_like(acc_ref)

    def step(i, carry):
        total = acc_ref[...]
        for j in range(per_step):
            q = i * per_step + j
            head, rest = split(sorted_ref[pl.ds(q, nact, stride=naux), :])
            b_head, b_rest = split(b_ref[q])
            both = jnp.dot(jnp.concatenate([head, rest]), b_head, preferred_element_type=jnp.float32)
            total += jnp.dot(head, b_rest, preferred_element_type=jnp.float32) + both[:nact] + both[nact:]
        acc_ref[...] = total
        return carry

    lax.fori_loop(0, steps, step, 0)
    half, lanes = out_ref.shape[1:]
    norb = acc_ref.shape[1]
    for h in range(2):
        for j in range(NX):
            wide = min(lanes, norb - j * lanes)
            if wide < lanes:
                out_ref[h * NX + j] = jnp.zeros((half, lanes), jnp.float32)
            out_ref[h * NX + j, :, :wide] = acc_ref[h * half : (h + 1) * half, j * lanes : j * lanes + wide]


def fock_product(fitted, b_tensor, lanes):
    naux, nact, norb = b_tensor.shape
    per_step = 8
    flat = [piece for group in fitted for piece in group]
    vmem = pl.BlockSpec(memory_space=pltpu.VMEM)
    return pl.pallas_call(
        functools.partial(fock_kernel, [len(group) for group in fitted], nact, per_step),
        out_shape=jax.ShapeDtypeStruct((2 * NX, nact // 2, lanes), jnp.float32),
        in_specs=[vmem] * (len(flat) + 1),
        out_specs=vmem,
        scratch_shapes=[
            pltpu.VMEM((nact * naux, nact), jnp.float32),
            pltpu.VMEM((nact, norb), jnp.float32),
        ],
        compiler_params=pltpu.CompilerParams(vmem_limit_bytes=16 * 2**20),
    )(*flat, b_tensor)


def grad_kernel(tiles_ref, gen_ref, grad_ref, packed_ref):
    half, lanes = tiles_ref.shape[1:]
    nact, norb = grad_ref.shape
    for h in range(2):
        for j in range(NX):
            wide = min(lanes, norb - j * lanes)
            grad_ref[h * half : (h + 1) * half, j * lanes : j * lanes + wide] = 2.0 * tiles_ref[h * NX + j, :, :wide]
    grad = grad_ref[...]
    packed_ref[:nact, :] = product(split(grad), split(gen_ref[...]), (((1,), (0,)), ((), ())))
    rows, cols = packed_ref.shape
    packed_ref[nact:, :] = jnp.zeros((rows - nact, cols), jnp.float32) + jnp.sum(grad * grad)


def general_kernel(grad_ref, act_ref, out_ref):
    out_ref[...] = product(split(grad_ref[...].T), split(act_ref[...]), (((1,), (0,)), ((), ())))


def scale_kernel(step_scale, whole_scale, a_ref, b_ref, c_ref, d_ref, grad_ref, raw_ref, dir_ref, act_ref, gen_ref):
    total = (a_ref[...] + c_ref[...]) + (b_ref[...] + d_ref[...])
    nact = act_ref.shape[0]
    inverse = 1.0 / jnp.sqrt(total[nact : nact + 1, 0:1] + 1e-06)
    dir_ref[...] = (whole_scale * inverse) * grad_ref[...]
    act_ref[...] = (-step_scale * inverse) * total[:nact]
    gen_ref[...] = (step_scale * inverse) * raw_ref[...]


def tail(tiles, gen_coeffs, act_coeffs, norb):
    nact = act_coeffs.shape[1]
    nbas = gen_coeffs.shape[0]
    f32 = jnp.float32
    shape = jax.ShapeDtypeStruct
    grad, packed = pl.pallas_call(
        grad_kernel, out_shape=(shape((nact, norb), f32), shape((nact + 8, nbas), f32)), compiler_params=SMALL
    )(tiles, gen_coeffs.T)
    raw = pl.pallas_call(general_kernel, out_shape=shape((norb, nbas), f32), compiler_params=SMALL)(grad, act_coeffs.T)
    packed = packed + swap_core(packed)
    others = [swap(packed, X, NX, mask) for mask in (1, 2, 3)]
    direction, active, general = pl.pallas_call(
        functools.partial(scale_kernel, math.sqrt(nact), math.sqrt(nact * norb * 2 * NX)),
        out_shape=(shape((nact, norb), f32), shape((nact, nbas), f32), shape((norb, nbas), f32)),
        compiler_params=SMALL,
    )(packed, *others, grad, raw)
    return direction, active.T, general.T


def on_device(pair_coeffs, rdm, b_tensor, gen_coeffs, act_coeffs):
    naux, nact, norb = b_tensor.shape
    half = naux // 2
    rows = [rdm, swap(rdm, "y", NY, 1)]
    near = {0: pair_coeffs}
    far = {0: swap(pair_coeffs, "y", NY, 3)}
    for k in range(1, NZ // 2):
        for found in (near, far):
            if found is near or k < 3:
                found[k] = shift(found[k - 1], "z", NZ, -1)
                found[NZ - k] = shift(found[(NZ - k + 1) % NZ], "z", NZ, 1)
    near[4] = shift(near[2], "z", NZ, -2)
    for k in (3, 5, 4):
        far[k] = swap(near[k], "y", NY, 3)

    kept, sent, *rows = pair_product([near[k] for k in range(NZ)], rows, True)
    chunks = [kept, swap_core(sent)]
    kept, sent = pair_product([far[(k + TURN) % NZ] for k in range(NZ)], rows, False)
    chunks += [kept, swap_core(sent)]
    first, second = sum_over_x(chunks)

    def rank(yy, zz, xx, cc):
        return (((yy * NZ + zz % NZ) * 2 + xx // 2) * 2 + cc) * 2 + xx % 2

    def send_home(value, mask, turn):
        pairs = [
            (rank(yy, zz, xx, cc), rank(yy ^ mask, zz + xx + NX * cc + turn, xx, cc))
            for yy in range(NY)
            for zz in range(NZ)
            for xx in range(NX)
            for cc in range(2)
        ]
        return lax.ppermute(value, ("y", "z", "xh", "co", "xl"), pairs)

    returned = pl.pallas_call(
        lanes_kernel,
        out_shape=jax.ShapeDtypeStruct((naux, 2 * first.shape[1]), first.dtype),
        compiler_params=SMALL,
    )(send_home(first, 0, 0), send_home(second, 3, TURN))

    after = shift(returned, X, NX, -1)
    before = shift(returned, X, NX, 1)
    far_low = shift(after[:half], X, NX, -1)
    far_high = shift(before[half:], X, NX, 1)
    mine = [[returned], [after], [far_low, far_high], [before]]
    theirs = [[swap_core(piece) for piece in group] for group in mine]

    lanes = 128 if norb > 128 else norb // NX
    tiles = fock_product(mine + theirs, b_tensor, lanes)
    piece = jnp.sum(lax.all_to_all(tiles, "z", split_axis=0, concat_axis=0, tiled=True), axis=0)
    piece = (piece + swap(piece, "y", NY, 2)) + (swap(piece, "y", NY, 1) + swap(piece, "y", NY, 3))
    tiles = lax.all_to_all(
        jnp.broadcast_to(piece[None], tiles.shape), "z", split_axis=0, concat_axis=0, tiled=True
    )
    return tail(tiles, gen_coeffs, act_coeffs, norb)


def solution(mesh):
    grid = Mesh(mesh.devices.reshape(NY, NZ, 2, 2, 2), ("y", "z", "xh", "co", "xl"))
    aux, cols = ("y", "z"), ("xh", "co", "xl")
    return jax.shard_map(
        on_device,
        mesh=grid,
        in_specs=(P(aux, cols), P(aux, cols), P(aux, None, cols), P(aux, cols), P(aux, None)),
        out_specs=(P(None, cols), P(aux, None), P(aux, cols)),
        check_vma=False,
    )
```

```python
import functools
import math

import jax
import jax.numpy as jnp
from jax import lax
from jax.experimental import pallas as pl
from jax.experimental.pallas import tpu as pltpu
from jax.sharding import Mesh, PartitionSpec as P

NY, NZ, NX = 4, 8, 4
TURN = 2
X = ("xh", "xl")
SMALL = pltpu.CompilerParams(vmem_limit_bytes=8 * 2**20)


def shift(value, axis, size, step):
    return lax.ppermute(value, axis, [(i, (i + step) % size) for i in range(size)])


def swap_core(value):
    return lax.ppermute(value, "co", [(0, 1), (1, 0)])


def swap(value, axis, size, mask):
    return lax.ppermute(value, axis, [(i, i ^ mask) for i in range(size)])


def split(value):
    head = value.astype(jnp.bfloat16)
    return head, (value - head.astype(jnp.float32)).astype(jnp.bfloat16)


def position():
    return lax.axis_index("y"), lax.axis_index("z"), lax.axis_index("xh") * 2 + lax.axis_index("xl"), lax.axis_index("co")


def product(left, right, dims):
    head, rest = left
    first, second = right
    total = lax.dot_general(head, first, dims, preferred_element_type=jnp.float32)
    total += lax.dot_general(head, second, dims, preferred_element_type=jnp.float32)
    return total + lax.dot_general(rest, first, dims, preferred_element_type=jnp.float32)


def pair_kernel(n_p, fresh, *refs):
    p_head, p_rest = refs[-2:]
    p_refs = refs[:n_p]
    if fresh:
        r_refs, (kept_ref, sent_ref, r_head, r_rest) = refs[n_p:-6], refs[-6:-2]
        start = 0
        for ref in r_refs:
            rows = ref.shape[0]
            r_head[start : start + rows, :], r_rest[start : start + rows, :] = split(ref[...])
            start += rows
    else:
        r_head, r_rest, kept_ref, sent_ref = refs[n_p:-2]
    _, _, x, core = position()
    half, n_cols = kept_ref.shape
    for k, ref in enumerate(p_refs):
        rows = ref.shape[0]
        start = ((k // NX) ^ core) * half + ((k % NX - x) & (NX - 1)) * rows
        place = pl.ds(pl.multiple_of(start, 16), rows)
        p_head[place, :], p_rest[place, :] = split(ref[...])
    for low in range(0, n_cols, 256):
        high = min(low + 256, n_cols)
        pieces = (r_head[low:high, :], r_rest[low:high, :])
        total = product((p_head[...], p_rest[...]), pieces, (((1,), (1,)), ((), ())))
        kept_ref[:, low:high] = total[:half]
        sent_ref[:, low:high] = total[half:]


def pair_product(p_pieces, rows, fresh):
    depth = p_pieces[0].shape[1]
    n_rows = sum(p.shape[0] for p in p_pieces)
    n_cols = sum(r.shape[0] for r in rows) if fresh else rows[0].shape[0]
    shape = jax.ShapeDtypeStruct((n_rows // 2, n_cols), jnp.float32)
    parts = jax.ShapeDtypeStruct((n_cols, depth), jnp.bfloat16)
    return pl.pallas_call(
        functools.partial(pair_kernel, len(p_pieces), fresh),
        out_shape=(shape, shape) + ((parts, parts) if fresh else ()),
        scratch_shapes=[pltpu.VMEM((n_rows, depth), jnp.bfloat16)] * 2,
        compiler_params=pltpu.CompilerParams(vmem_limit_bytes=16 * 2**20),
        cost_estimate=pl.CostEstimate(
            flops=1000 if fresh else 6 * n_rows * n_cols * depth,
            bytes_accessed=1000 if fresh else 4 * (n_rows + n_cols) * depth,
            transcendentals=0,
        ),
    )(*p_pieces, *rows)


def join_kernel(*refs):
    chunks, (own_ref, after_ref, before_ref, low_ref, high_ref) = refs[:-5], refs[-5:]
    rows = own_ref.shape[0]
    start = 0
    for kept_ref, got_ref in zip(chunks[::2], chunks[1::2]):
        lanes = slice(start, start + kept_ref.shape[1])
        start = lanes.stop
        total = kept_ref[...] + got_ref[...]
        own_ref[:, lanes] = total[:rows]
        after_ref[:, lanes] = total[rows : 2 * rows]
        low_ref[:, lanes] = total[2 * rows : 2 * rows + rows // 2]
        high_ref[:, lanes] = total[2 * rows + rows // 2 : 3 * rows]
        before_ref[:, lanes] = total[3 * rows :]


def add_kernel(after_ref, up_ref, before_ref, down_ref, after_out, before_out):
    half = up_ref.shape[0]
    after_out[:half] = after_ref[:half] + up_ref[...]
    after_out[half:] = after_ref[half:]
    before_out[:half] = before_ref[:half]
    before_out[half:] = before_ref[half:] + down_ref[...]


def sides_kernel(own_ref, one_ref, two_ref, first_ref, second_ref):
    total = own_ref[...] + one_ref[...] + two_ref[...]
    lanes = first_ref.shape[1]
    first_ref[...] = total[:, :lanes]
    second_ref[...] = total[:, lanes:]


def lanes_kernel(first_ref, second_ref, out_ref):
    lanes = first_ref.shape[1]
    out_ref[:, :lanes] = first_ref[...]
    out_ref[:, lanes:] = second_ref[...]


def sum_over_x(chunks):
    rows = chunks[0].shape[0] // NX
    lanes = sum(chunk.shape[1] for chunk in chunks[::2])
    whole, part = (jax.ShapeDtypeStruct((n, lanes), jnp.float32) for n in (rows, rows // 2))
    own, after, before, low, high = pl.pallas_call(
        join_kernel, out_shape=(whole, whole, whole, part, part), compiler_params=SMALL
    )(*chunks)
    up, down = shift(low, X, NX, 1), shift(high, X, NX, -1)
    after, before = pl.pallas_call(add_kernel, out_shape=(whole, whole), compiler_params=SMALL)(after, up, before, down)
    side = jax.ShapeDtypeStruct((rows, lanes // 2), jnp.float32)
    return pl.pallas_call(sides_kernel, out_shape=(side, side), compiler_params=SMALL)(
        own, shift(after, X, NX, 1), shift(before, X, NX, -1)
    )


def fock_kernel(sizes, nact, per_step, *refs):
    b_ref, out_ref, sorted_ref, acc_ref = refs[-4:]
    y, z, x, core = position()
    naux = b_ref.shape[0]
    steps = naux // per_step

    n_t = refs[0].shape[1] // nact // NY
    at = 0
    for g, size in enumerate(sizes):
        c, s = g // NX, g % NX
        zb = (z - ((x + s) & (NX - 1)) - NX * ((core + c) & 1)) & (NZ - 1)
        base = 0
        for ref in refs[at : at + size]:
            rows = ref.shape[0]
            for j, mask in enumerate((0, 1, 3, 2)):
                turned = zb if j < 2 else (zb - TURN) & (NZ - 1)
                first = ((y ^ mask) * NZ + turned) * n_t
                for t in range(n_t):
                    place = pl.ds(pl.multiple_of((first + t) * naux + base, 8), rows)
                    low = (j * n_t + t) * nact
                    sorted_ref[place, :] = ref[:, low : low + nact]
            base += rows
        at += size
    acc_ref[...] = jnp.zeros_like(acc_ref)

    def step(i, carry):
        total = acc_ref[...]
        for j in range(0, per_step, 2):
            q = i * per_step + j
            left = [sorted_ref[pl.ds(q + side, nact, stride=naux), :] for side in range(2)]
            head, rest = split(jnp.concatenate(left, axis=1))
            b_head, b_rest = split(b_ref[pl.ds(q, 2)].reshape(2 * nact, b_ref.shape[2]))
            both = jnp.dot(jnp.concatenate([head, rest]), b_head, preferred_element_type=jnp.float32)
            total += jnp.dot(head, b_rest, preferred_element_type=jnp.float32) + both[:nact] + both[nact:]
        acc_ref[...] = total
        return carry

    lax.fori_loop(0, steps, step, 0)
    half, lanes = out_ref.shape[1:]
    norb = acc_ref.shape[1]
    for h in range(2):
        for j in range(NX):
            wide = min(lanes, norb - j * lanes)
            if wide < lanes:
                out_ref[h * NX + j] = jnp.zeros((half, lanes), jnp.float32)
            out_ref[h * NX + j, :, :wide] = acc_ref[h * half : (h + 1) * half, j * lanes : j * lanes + wide]


def fock_product(fitted, b_tensor, lanes):
    naux, nact, norb = b_tensor.shape
    per_step = 8
    flat = [piece for group in fitted for piece in group]
    vmem = pl.BlockSpec(memory_space=pltpu.VMEM)
    return pl.pallas_call(
        functools.partial(fock_kernel, [len(group) for group in fitted], nact, per_step),
        out_shape=jax.ShapeDtypeStruct((2 * NX, nact // 2, lanes), jnp.float32),
        in_specs=[vmem] * (len(flat) + 1),
        out_specs=vmem,
        scratch_shapes=[
            pltpu.VMEM((nact * naux, nact), jnp.float32),
            pltpu.VMEM((nact, norb), jnp.float32),
        ],
        compiler_params=pltpu.CompilerParams(vmem_limit_bytes=16 * 2**20),
    )(*flat, b_tensor)


def grad_kernel(tiles_ref, gen_ref, grad_ref, packed_ref):
    half, lanes = tiles_ref.shape[1:]
    nact, norb = grad_ref.shape
    for h in range(2):
        for j in range(NX):
            wide = min(lanes, norb - j * lanes)
            grad_ref[h * half : (h + 1) * half, j * lanes : j * lanes + wide] = 2.0 * tiles_ref[h * NX + j, :, :wide]
    grad = grad_ref[...]
    packed_ref[:nact, :] = product(split(grad), split(gen_ref[...]), (((1,), (0,)), ((), ())))
    rows, cols = packed_ref.shape
    packed_ref[nact:, :] = jnp.zeros((rows - nact, cols), jnp.float32) + jnp.sum(grad * grad)


def general_kernel(grad_ref, act_ref, out_ref):
    out_ref[...] = product(split(grad_ref[...].T), split(act_ref[...]), (((1,), (0,)), ((), ())))


def scale_kernel(step_scale, whole_scale, a_ref, b_ref, c_ref, d_ref, grad_ref, raw_ref, dir_ref, act_ref, gen_ref):
    total = (a_ref[...] + c_ref[...]) + (b_ref[...] + d_ref[...])
    nact = act_ref.shape[0]
    inverse = 1.0 / jnp.sqrt(total[nact : nact + 1, 0:1] + 1e-06)
    dir_ref[...] = (whole_scale * inverse) * grad_ref[...]
    act_ref[...] = (-step_scale * inverse) * total[:nact]
    gen_ref[...] = (step_scale * inverse) * raw_ref[...]


def tail(tiles, gen_coeffs, act_coeffs, norb):
    nact = act_coeffs.shape[1]
    nbas = gen_coeffs.shape[0]
    f32 = jnp.float32
    shape = jax.ShapeDtypeStruct
    grad, packed = pl.pallas_call(
        grad_kernel, out_shape=(shape((nact, norb), f32), shape((nact + 8, nbas), f32)), compiler_params=SMALL
    )(tiles, gen_coeffs.T)
    raw = pl.pallas_call(general_kernel, out_shape=shape((norb, nbas), f32), compiler_params=SMALL)(grad, act_coeffs.T)
    packed = packed + swap_core(packed)
    others = [swap(packed, X, NX, mask) for mask in (1, 2, 3)]
    direction, active, general = pl.pallas_call(
        functools.partial(scale_kernel, math.sqrt(nact), math.sqrt(nact * norb * 2 * NX)),
        out_shape=(shape((nact, norb), f32), shape((nact, nbas), f32), shape((norb, nbas), f32)),
        compiler_params=SMALL,
    )(packed, *others, grad, raw)
    return direction, active.T, general.T


def on_device(pair_coeffs, rdm, b_tensor, gen_coeffs, act_coeffs):
    naux, nact, norb = b_tensor.shape
    half = naux // 2
    rows = [rdm, swap(rdm, "y", NY, 1)]
    near = {0: pair_coeffs}
    far = {0: swap(pair_coeffs, "y", NY, 3)}
    for k in range(1, NZ // 2):
        for found in (near, far):
            if found is near or k < 3:
                found[k] = shift(found[k - 1], "z", NZ, -1)
                found[NZ - k] = shift(found[(NZ - k + 1) % NZ], "z", NZ, 1)
    near[4] = shift(near[3], "z", NZ, -1)
    for k in (3, 5, 4):
        far[k] = swap(near[k], "y", NY, 3)

    kept, sent, *rows = pair_product([near[k] for k in range(NZ)], rows, True)
    chunks = [kept, swap_core(sent)]
    kept, sent = pair_product([far[(k + TURN) % NZ] for k in range(NZ)], rows, False)
    chunks += [kept, swap_core(sent)]
    first, second = sum_over_x(chunks)

    def rank(yy, zz, xx, cc):
        return (((yy * NZ + zz % NZ) * 2 + xx // 2) * 2 + cc) * 2 + xx % 2

    def send_home(value, mask, turn):
        pairs = [
            (rank(yy, zz, xx, cc), rank(yy ^ mask, zz + xx + NX * cc + turn, xx, cc))
            for yy in range(NY)
            for zz in range(NZ)
            for xx in range(NX)
            for cc in range(2)
        ]
        return lax.ppermute(value, ("y", "z", "xh", "co", "xl"), pairs)

    returned = pl.pallas_call(
        lanes_kernel,
        out_shape=jax.ShapeDtypeStruct((naux, 2 * first.shape[1]), first.dtype),
        compiler_params=SMALL,
    )(send_home(first, 0, 0), send_home(second, 3, TURN))

    after = shift(returned, X, NX, -1)
    before = shift(returned, X, NX, 1)
    far_low = shift(after[:half], X, NX, -1)
    far_high = shift(before[half:], X, NX, 1)
    mine = [[returned], [after], [far_low, far_high], [before]]
    theirs = [[swap_core(piece) for piece in group] for group in mine]

    lanes = 128 if norb > 128 else norb // NX
    tiles = fock_product(mine + theirs, b_tensor, lanes)
    piece = jnp.sum(lax.all_to_all(tiles, "z", split_axis=0, concat_axis=0, tiled=True), axis=0)
    piece = (piece + swap(piece, "y", NY, 2)) + (swap(piece, "y", NY, 1) + swap(piece, "y", NY, 3))
    tiles = lax.all_to_all(
        jnp.broadcast_to(piece[None], tiles.shape), "z", split_axis=0, concat_axis=0, tiled=True
    )
    return tail(tiles, gen_coeffs, act_coeffs, norb)


def solution(mesh):
    grid = Mesh(mesh.devices.reshape(NY, NZ, 2, 2, 2), ("y", "z", "xh", "co", "xl"))
    aux, cols = ("y", "z"), ("xh", "co", "xl")
    return jax.shard_map(
        on_device,
        mesh=grid,
        in_specs=(P(aux, cols), P(aux, cols), P(aux, None, cols), P(aux, cols), P(aux, None)),
        out_specs=(P(None, cols), P(aux, None), P(aux, cols)),
        check_vma=False,
    )
```

```python
import functools
import math

import jax
import jax.numpy as jnp
from jax import lax
from jax.experimental import pallas as pl
from jax.experimental.pallas import tpu as pltpu
from jax.sharding import Mesh, PartitionSpec as P

NY, NZ, NX = 4, 8, 4
TURN = 2
X = ("xh", "xl")
SMALL = pltpu.CompilerParams(vmem_limit_bytes=8 * 2**20)


def shift(value, axis, size, step):
    return lax.ppermute(value, axis, [(i, (i + step) % size) for i in range(size)])


def swap_core(value):
    return lax.ppermute(value, "co", [(0, 1), (1, 0)])


def around(value, sign):
    pairs = [(z * 2 + c, (z - sign * (1 - 2 * c)) % NZ * 2 + c) for z in range(NZ) for c in range(2)]
    return lax.ppermute(value, ("z", "co"), pairs)


def swap(value, axis, size, mask):
    return lax.ppermute(value, axis, [(i, i ^ mask) for i in range(size)])


def split(value):
    head = value.astype(jnp.bfloat16)
    return head, (value - head.astype(jnp.float32)).astype(jnp.bfloat16)


def position():
    return lax.axis_index("y"), lax.axis_index("z"), lax.axis_index("xh") * 2 + lax.axis_index("xl"), lax.axis_index("co")


def product(left, right, dims):
    head, rest = left
    first, second = right
    total = lax.dot_general(head, first, dims, preferred_element_type=jnp.float32)
    total += lax.dot_general(head, second, dims, preferred_element_type=jnp.float32)
    return total + lax.dot_general(rest, first, dims, preferred_element_type=jnp.float32)


def pair_kernel(n_p, turn, fresh, *refs):
    p_head, p_rest = refs[-2:]
    p_refs = refs[:n_p]
    if fresh:
        r_refs, (kept_ref, sent_ref, r_head, r_rest) = refs[n_p:-6], refs[-6:-2]
        start = 0
        for ref in r_refs:
            rows = ref.shape[0]
            r_head[start : start + rows, :], r_rest[start : start + rows, :] = split(ref[...])
            start += rows
    else:
        r_head, r_rest, kept_ref, sent_ref = refs[n_p:-2]
    _, _, x, core = position()
    half, n_cols = kept_ref.shape
    for k, ref in enumerate(p_refs):
        rows = ref.shape[0]
        offset = (k * (1 - 2 * core) - turn) & (NZ - 1)
        start = ((offset >> 2) ^ core) * half + ((offset - x) & (NX - 1)) * rows
        place = pl.ds(pl.multiple_of(start, 16), rows)
        p_head[place, :], p_rest[place, :] = split(ref[...])
    for low in range(0, n_cols, 256):
        high = min(low + 256, n_cols)
        pieces = (r_head[low:high, :], r_rest[low:high, :])
        total = product((p_head[...], p_rest[...]), pieces, (((1,), (1,)), ((), ())))
        kept_ref[:, low:high] = total[:half]
        sent_ref[:, low:high] = total[half:]


def pair_product(p_pieces, rows, turn, fresh):
    depth = p_pieces[0].shape[1]
    n_rows = sum(p.shape[0] for p in p_pieces)
    n_cols = sum(r.shape[0] for r in rows) if fresh else rows[0].shape[0]
    shape = jax.ShapeDtypeStruct((n_rows // 2, n_cols), jnp.float32)
    parts = jax.ShapeDtypeStruct((n_cols, depth), jnp.bfloat16)
    return pl.pallas_call(
        functools.partial(pair_kernel, len(p_pieces), turn, fresh),
        out_shape=(shape, shape) + ((parts, parts) if fresh else ()),
        scratch_shapes=[pltpu.VMEM((n_rows, depth), jnp.bfloat16)] * 2,
        compiler_params=pltpu.CompilerParams(vmem_limit_bytes=16 * 2**20),
        cost_estimate=pl.CostEstimate(
            flops=1000 if fresh else 6 * n_rows * n_cols * depth,
            bytes_accessed=1000 if fresh else 4 * (n_rows + n_cols) * depth,
            transcendentals=0,
        ),
    )(*p_pieces, *rows)


def join_kernel(*refs):
    chunks, (own_ref, after_ref, before_ref, low_ref, high_ref) = refs[:-5], refs[-5:]
    rows = own_ref.shape[0]
    start = 0
    for kept_ref, got_ref in zip(chunks[::2], chunks[1::2]):
        lanes = slice(start, start + kept_ref.shape[1])
        start = lanes.stop
        total = kept_ref[...] + got_ref[...]
        own_ref[:, lanes] = total[:rows]
        after_ref[:, lanes] = total[rows : 2 * rows]
        low_ref[:, lanes] = total[2 * rows : 2 * rows + rows // 2]
        high_ref[:, lanes] = total[2 * rows + rows // 2 : 3 * rows]
        before_ref[:, lanes] = total[3 * rows :]


def add_kernel(after_ref, up_ref, before_ref, down_ref, after_out, before_out):
    half = up_ref.shape[0]
    after_out[:half] = after_ref[:half] + up_ref[...]
    after_out[half:] = after_ref[half:]
    before_out[:half] = before_ref[:half]
    before_out[half:] = before_ref[half:] + down_ref[...]


def sides_kernel(own_ref, one_ref, two_ref, first_ref, second_ref):
    total = own_ref[...] + one_ref[...] + two_ref[...]
    lanes = first_ref.shape[1]
    first_ref[...] = total[:, :lanes]
    second_ref[...] = total[:, lanes:]


def lanes_kernel(first_ref, second_ref, out_ref):
    lanes = first_ref.shape[1]
    out_ref[:, :lanes] = first_ref[...]
    out_ref[:, lanes:] = second_ref[...]


def sum_over_x(chunks):
    rows = chunks[0].shape[0] // NX
    lanes = sum(chunk.shape[1] for chunk in chunks[::2])
    whole, part = (jax.ShapeDtypeStruct((n, lanes), jnp.float32) for n in (rows, rows // 2))
    own, after, before, low, high = pl.pallas_call(
        join_kernel, out_shape=(whole, whole, whole, part, part), compiler_params=SMALL
    )(*chunks)
    up, down = shift(low, X, NX, 1), shift(high, X, NX, -1)
    after, before = pl.pallas_call(add_kernel, out_shape=(whole, whole), compiler_params=SMALL)(after, up, before, down)
    side = jax.ShapeDtypeStruct((rows, lanes // 2), jnp.float32)
    return pl.pallas_call(sides_kernel, out_shape=(side, side), compiler_params=SMALL)(
        own, shift(after, X, NX, 1), shift(before, X, NX, -1)
    )


def fock_kernel(sizes, nact, per_step, *refs):
    b_ref, out_ref, sorted_ref, acc_ref = refs[-4:]
    y, z, x, core = position()
    naux = b_ref.shape[0]
    steps = naux // per_step

    n_t = refs[0].shape[1] // nact // NY
    at = 0
    for g, size in enumerate(sizes):
        c, s = g // NX, g % NX
        zb = (z - ((x + s) & (NX - 1)) - NX * ((core + c) & 1)) & (NZ - 1)
        base = 0
        for ref in refs[at : at + size]:
            rows = ref.shape[0]
            for j, mask in enumerate((0, 1, 3, 2)):
                turned = zb if j < 2 else (zb - TURN) & (NZ - 1)
                first = ((y ^ mask) * NZ + turned) * n_t
                for t in range(n_t):
                    place = pl.ds(pl.multiple_of((first + t) * naux + base, 8), rows)
                    low = (j * n_t + t) * nact
                    sorted_ref[place, :] = ref[:, low : low + nact]
            base += rows
        at += size
    acc_ref[...] = jnp.zeros_like(acc_ref)

    def step(i, carry):
        total = acc_ref[...]
        for j in range(0, per_step, 2):
            q = i * per_step + j
            left = [sorted_ref[pl.ds(q + side, nact, stride=naux), :] for side in range(2)]
            head, rest = split(jnp.concatenate(left, axis=1))
            b_head, b_rest = split(b_ref[pl.ds(q, 2)].reshape(2 * nact, b_ref.shape[2]))
            both = jnp.dot(jnp.concatenate([head, rest]), b_head, preferred_element_type=jnp.float32)
            total += jnp.dot(head, b_rest, preferred_element_type=jnp.float32) + both[:nact] + both[nact:]
        acc_ref[...] = total
        return carry

    lax.fori_loop(0, steps, step, 0)
    half, lanes = out_ref.shape[1:]
    norb = acc_ref.shape[1]
    for h in range(2):
        for j in range(NX):
            wide = min(lanes, norb - j * lanes)
            if wide < lanes:
                out_ref[h * NX + j] = jnp.zeros((half, lanes), jnp.float32)
            out_ref[h * NX + j, :, :wide] = acc_ref[h * half : (h + 1) * half, j * lanes : j * lanes + wide]


def fock_product(fitted, b_tensor, lanes):
    naux, nact, norb = b_tensor.shape
    per_step = 8
    flat = [piece for group in fitted for piece in group]
    vmem = pl.BlockSpec(memory_space=pltpu.VMEM)
    return pl.pallas_call(
        functools.partial(fock_kernel, [len(group) for group in fitted], nact, per_step),
        out_shape=jax.ShapeDtypeStruct((2 * NX, nact // 2, lanes), jnp.float32),
        in_specs=[vmem] * (len(flat) + 1),
        out_specs=vmem,
        scratch_shapes=[
            pltpu.VMEM((nact * naux, nact), jnp.float32),
            pltpu.VMEM((nact, norb), jnp.float32),
        ],
        compiler_params=pltpu.CompilerParams(vmem_limit_bytes=16 * 2**20),
    )(*flat, b_tensor)


def grad_kernel(tiles_ref, gen_ref, grad_ref, packed_ref):
    half, lanes = tiles_ref.shape[1:]
    nact, norb = grad_ref.shape
    for h in range(2):
        for j in range(NX):
            wide = min(lanes, norb - j * lanes)
            grad_ref[h * half : (h + 1) * half, j * lanes : j * lanes + wide] = 2.0 * tiles_ref[h * NX + j, :, :wide]
    grad = grad_ref[...]
    packed_ref[:nact, :] = product(split(grad), split(gen_ref[...]), (((1,), (0,)), ((), ())))
    rows, cols = packed_ref.shape
    packed_ref[nact:, :] = jnp.zeros((rows - nact, cols), jnp.float32) + jnp.sum(grad * grad)


def general_kernel(grad_ref, act_ref, out_ref):
    out_ref[...] = product(split(grad_ref[...].T), split(act_ref[...]), (((1,), (0,)), ((), ())))


def scale_kernel(step_scale, whole_scale, a_ref, b_ref, c_ref, d_ref, grad_ref, raw_ref, dir_ref, act_ref, gen_ref):
    total = (a_ref[...] + c_ref[...]) + (b_ref[...] + d_ref[...])
    nact = act_ref.shape[0]
    inverse = 1.0 / jnp.sqrt(total[nact : nact + 1, 0:1] + 1e-06)
    dir_ref[...] = (whole_scale * inverse) * grad_ref[...]
    act_ref[...] = (-step_scale * inverse) * total[:nact]
    gen_ref[...] = (step_scale * inverse) * raw_ref[...]


def tail(tiles, gen_coeffs, act_coeffs, norb):
    nact = act_coeffs.shape[1]
    nbas = gen_coeffs.shape[0]
    f32 = jnp.float32
    shape = jax.ShapeDtypeStruct
    grad, packed = pl.pallas_call(
        grad_kernel, out_shape=(shape((nact, norb), f32), shape((nact + 8, nbas), f32)), compiler_params=SMALL
    )(tiles, gen_coeffs.T)
    raw = pl.pallas_call(general_kernel, out_shape=shape((norb, nbas), f32), compiler_params=SMALL)(grad, act_coeffs.T)
    packed = packed + swap_core(packed)
    others = [swap(packed, X, NX, mask) for mask in (1, 2, 3)]
    direction, active, general = pl.pallas_call(
        functools.partial(scale_kernel, math.sqrt(nact), math.sqrt(nact * norb * 2 * NX)),
        out_shape=(shape((nact, norb), f32), shape((nact, nbas), f32), shape((norb, nbas), f32)),
        compiler_params=SMALL,
    )(packed, *others, grad, raw)
    return direction, active.T, general.T


def on_device(pair_coeffs, rdm, b_tensor, gen_coeffs, act_coeffs):
    naux, nact, norb = b_tensor.shape
    half = naux // 2
    rows = [rdm, swap(rdm, "y", NY, 1)]
    near = {0: pair_coeffs}
    far = {0: swap(pair_coeffs, "y", NY, 3)}
    for k in range(1, NZ // 2):
        for found in (near, far):
            if found is near or k < 3:
                found[k] = around(found[k - 1], 1)
                found[NZ - k] = around(found[(NZ - k + 1) % NZ], -1)
    near[4] = around(near[3], 1)
    for k in (3, 5, 4):
        far[k] = swap(near[k], "y", NY, 3)

    kept, sent, *rows = pair_product([near[k] for k in range(NZ)], rows, 0, True)
    chunks = [kept, swap_core(sent)]
    kept, sent = pair_product([far[k] for k in range(NZ)], rows, TURN, False)
    chunks += [kept, swap_core(sent)]
    first, second = sum_over_x(chunks)

    def rank(yy, zz, xx, cc):
        return (((yy * NZ + zz % NZ) * 2 + xx // 2) * 2 + cc) * 2 + xx % 2

    def send_home(value, mask, turn):
        pairs = [
            (rank(yy, zz, xx, cc), rank(yy ^ mask, zz + xx + NX * cc + turn, xx, cc))
            for yy in range(NY)
            for zz in range(NZ)
            for xx in range(NX)
            for cc in range(2)
        ]
        return lax.ppermute(value, ("y", "z", "xh", "co", "xl"), pairs)

    returned = pl.pallas_call(
        lanes_kernel,
        out_shape=jax.ShapeDtypeStruct((naux, 2 * first.shape[1]), first.dtype),
        compiler_params=SMALL,
    )(send_home(first, 0, 0), send_home(second, 3, TURN))

    after = shift(returned, X, NX, -1)
    before = shift(returned, X, NX, 1)
    far_low = shift(after[:half], X, NX, -1)
    far_high = shift(before[half:], X, NX, 1)
    mine = [[returned], [after], [far_low, far_high], [before]]
    theirs = [[swap_core(piece) for piece in group] for group in mine]

    lanes = 128 if norb > 128 else norb // NX
    tiles = fock_product(mine + theirs, b_tensor, lanes)
    piece = jnp.sum(lax.all_to_all(tiles, "z", split_axis=0, concat_axis=0, tiled=True), axis=0)
    piece = (piece + swap(piece, "y", NY, 2)) + (swap(piece, "y", NY, 1) + swap(piece, "y", NY, 3))
    tiles = lax.all_to_all(
        jnp.broadcast_to(piece[None], tiles.shape), "z", split_axis=0, concat_axis=0, tiled=True
    )
    return tail(tiles, gen_coeffs, act_coeffs, norb)


def solution(mesh):
    grid = Mesh(mesh.devices.reshape(NY, NZ, 2, 2, 2), ("y", "z", "xh", "co", "xl"))
    aux, cols = ("y", "z"), ("xh", "co", "xl")
    return jax.shard_map(
        on_device,
        mesh=grid,
        in_specs=(P(aux, cols), P(aux, cols), P(aux, None, cols), P(aux, cols), P(aux, None)),
        out_specs=(P(None, cols), P(aux, None), P(aux, cols)),
        check_vma=False,
    )
```

```python
import functools
import math

import jax
import jax.numpy as jnp
from jax import lax
from jax.experimental import pallas as pl
from jax.experimental.pallas import tpu as pltpu
from jax.sharding import Mesh, PartitionSpec as P

NY, NZ, NX = 4, 8, 4
TURN = 2
X = ("xh", "xl")
SMALL = pltpu.CompilerParams(vmem_limit_bytes=8 * 2**20)


def shift(value, axis, size, step):
    return lax.ppermute(value, axis, [(i, (i + step) % size) for i in range(size)])


def swap_core(value):
    return lax.ppermute(value, "co", [(0, 1), (1, 0)])


def swap(value, axis, size, mask):
    return lax.ppermute(value, axis, [(i, i ^ mask) for i in range(size)])


def split(value):
    head = value.astype(jnp.bfloat16)
    return head, (value - head.astype(jnp.float32)).astype(jnp.bfloat16)


def position():
    return lax.axis_index("y"), lax.axis_index("z"), lax.axis_index("xh") * 2 + lax.axis_index("xl"), lax.axis_index("co")


def product(left, right, dims):
    head, rest = left
    first, second = right
    total = lax.dot_general(head, first, dims, preferred_element_type=jnp.float32)
    total += lax.dot_general(head, second, dims, preferred_element_type=jnp.float32)
    return total + lax.dot_general(rest, first, dims, preferred_element_type=jnp.float32)


def pair_kernel(n_p, fresh, *refs):
    p_head, p_rest = refs[-2:]
    p_refs = refs[:n_p]
    if fresh:
        r_refs, (kept_ref, sent_ref, r_head, r_rest) = refs[n_p:-6], refs[-6:-2]
        start = 0
        for ref in r_refs:
            rows = ref.shape[0]
            r_head[start : start + rows, :], r_rest[start : start + rows, :] = split(ref[...])
            start += rows
    else:
        r_head, r_rest, kept_ref, sent_ref = refs[n_p:-2]
    _, _, x, core = position()
    half, n_cols = kept_ref.shape
    for k, ref in enumerate(p_refs):
        rows = ref.shape[0]
        start = ((k // NX) ^ core) * half + ((k % NX - x) & (NX - 1)) * rows
        place = pl.ds(pl.multiple_of(start, 16), rows)
        p_head[place, :], p_rest[place, :] = split(ref[...])
    for low in range(0, n_cols, 256):
        high = min(low + 256, n_cols)
        pieces = (r_head[low:high, :], r_rest[low:high, :])
        total = product((p_head[...], p_rest[...]), pieces, (((1,), (1,)), ((), ())))
        kept_ref[:, low:high] = total[:half]
        sent_ref[:, low:high] = total[half:]


def pair_product(p_pieces, rows, fresh):
    depth = p_pieces[0].shape[1]
    n_rows = sum(p.shape[0] for p in p_pieces)
    n_cols = sum(r.shape[0] for r in rows) if fresh else rows[0].shape[0]
    shape = jax.ShapeDtypeStruct((n_rows // 2, n_cols), jnp.float32)
    parts = jax.ShapeDtypeStruct((n_cols, depth), jnp.bfloat16)
    return pl.pallas_call(
        functools.partial(pair_kernel, len(p_pieces), fresh),
        out_shape=(shape, shape) + ((parts, parts) if fresh else ()),
        scratch_shapes=[pltpu.VMEM((n_rows, depth), jnp.bfloat16)] * 2,
        compiler_params=pltpu.CompilerParams(vmem_limit_bytes=16 * 2**20),
        cost_estimate=pl.CostEstimate(
            flops=1000 if fresh else 6 * n_rows * n_cols * depth,
            bytes_accessed=1000 if fresh else 4 * (n_rows + n_cols) * depth,
            transcendentals=0,
        ),
    )(*p_pieces, *rows)


def join_kernel(*refs):
    chunks, (own_ref, after_ref, before_ref, low_ref, high_ref) = refs[:-5], refs[-5:]
    rows = own_ref.shape[0]
    start = 0
    for kept_ref, got_ref in zip(chunks[::2], chunks[1::2]):
        lanes = slice(start, start + kept_ref.shape[1])
        start = lanes.stop
        total = kept_ref[...] + got_ref[...]
        own_ref[:, lanes] = total[:rows]
        after_ref[:, lanes] = total[rows : 2 * rows]
        low_ref[:, lanes] = total[2 * rows : 2 * rows + rows // 2]
        high_ref[:, lanes] = total[2 * rows + rows // 2 : 3 * rows]
        before_ref[:, lanes] = total[3 * rows :]


def add_kernel(after_ref, up_ref, before_ref, down_ref, after_out, before_out):
    half = up_ref.shape[0]
    after_out[:half] = after_ref[:half] + up_ref[...]
    after_out[half:] = after_ref[half:]
    before_out[:half] = before_ref[:half]
    before_out[half:] = before_ref[half:] + down_ref[...]


def sides_kernel(own_ref, one_ref, two_ref, first_ref, second_ref):
    total = own_ref[...] + one_ref[...] + two_ref[...]
    lanes = first_ref.shape[1]
    first_ref[...] = total[:, :lanes]
    second_ref[...] = total[:, lanes:]


def lanes_kernel(first_ref, second_ref, out_ref):
    lanes = first_ref.shape[1]
    out_ref[:, :lanes] = first_ref[...]
    out_ref[:, lanes:] = second_ref[...]


def sum_over_x(chunks):
    rows = chunks[0].shape[0] // NX
    lanes = sum(chunk.shape[1] for chunk in chunks[::2])
    whole, part = (jax.ShapeDtypeStruct((n, lanes), jnp.float32) for n in (rows, rows // 2))
    own, after, before, low, high = pl.pallas_call(
        join_kernel, out_shape=(whole, whole, whole, part, part), compiler_params=SMALL
    )(*chunks)
    up, down = shift(low, X, NX, 1), shift(high, X, NX, -1)
    after, before = pl.pallas_call(add_kernel, out_shape=(whole, whole), compiler_params=SMALL)(after, up, before, down)
    side = jax.ShapeDtypeStruct((rows, lanes // 2), jnp.float32)
    return pl.pallas_call(sides_kernel, out_shape=(side, side), compiler_params=SMALL)(
        own, shift(after, X, NX, 1), shift(before, X, NX, -1)
    )


def fock_kernel(sizes, nact, per_step, *refs):
    b_ref, out_ref, sorted_ref, acc_ref = refs[-4:]
    y, z, x, core = position()
    naux = b_ref.shape[0]
    steps = naux // per_step

    n_t = refs[0].shape[1] // nact // NY
    at = 0
    for g, size in enumerate(sizes):
        c, s = g // NX, g % NX
        zb = (z - ((x + s) & (NX - 1)) - NX * ((core + c) & 1)) & (NZ - 1)
        base = 0
        for ref in refs[at : at + size]:
            rows = ref.shape[0]
            for j, mask in enumerate((0, 1, 3, 2)):
                turned = zb if j < 2 else (zb - TURN) & (NZ - 1)
                first = ((y ^ mask) * NZ + turned) * n_t
                for t in range(n_t):
                    place = pl.ds(pl.multiple_of((first + t) * naux + base, 8), rows)
                    low = (j * n_t + t) * nact
                    sorted_ref[place, :] = ref[:, low : low + nact]
            base += rows
        at += size
    acc_ref[...] = jnp.zeros_like(acc_ref)

    def step(i, carry):
        total = acc_ref[...]
        for j in range(0, per_step, 2):
            q = i * per_step + j
            left = [sorted_ref[pl.ds(q + side, nact, stride=naux), :] for side in range(2)]
            head, rest = split(jnp.concatenate(left, axis=1))
            b_head, b_rest = split(b_ref[pl.ds(q, 2)].reshape(2 * nact, b_ref.shape[2]))
            both = jnp.dot(jnp.concatenate([head, rest]), b_head, preferred_element_type=jnp.float32)
            total += jnp.dot(head, b_rest, preferred_element_type=jnp.float32) + both[:nact] + both[nact:]
        acc_ref[...] = total
        return carry

    lax.fori_loop(0, steps, step, 0)
    half, lanes = out_ref.shape[1:]
    norb = acc_ref.shape[1]
    for h in range(2):
        for j in range(NX):
            wide = min(lanes, norb - j * lanes)
            if wide < lanes:
                out_ref[h * NX + j] = jnp.zeros((half, lanes), jnp.float32)
            out_ref[h * NX + j, :, :wide] = acc_ref[h * half : (h + 1) * half, j * lanes : j * lanes + wide]


def fock_product(fitted, b_tensor, lanes):
    naux, nact, norb = b_tensor.shape
    per_step = 8
    flat = [piece for group in fitted for piece in group]
    vmem = pl.BlockSpec(memory_space=pltpu.VMEM)
    return pl.pallas_call(
        functools.partial(fock_kernel, [len(group) for group in fitted], nact, per_step),
        out_shape=jax.ShapeDtypeStruct((2 * NX, nact // 2, lanes), jnp.float32),
        in_specs=[vmem] * (len(flat) + 1),
        out_specs=vmem,
        scratch_shapes=[
            pltpu.VMEM((nact * naux, nact), jnp.float32),
            pltpu.VMEM((nact, norb), jnp.float32),
        ],
        compiler_params=pltpu.CompilerParams(vmem_limit_bytes=16 * 2**20),
    )(*flat, b_tensor)


def grad_kernel(tiles_ref, gen_ref, grad_ref, packed_ref):
    half, lanes = tiles_ref.shape[1:]
    nact, norb = grad_ref.shape
    for h in range(2):
        for j in range(NX):
            wide = min(lanes, norb - j * lanes)
            grad_ref[h * half : (h + 1) * half, j * lanes : j * lanes + wide] = 2.0 * tiles_ref[h * NX + j, :, :wide]
    grad = grad_ref[...]
    packed_ref[:nact, :] = product(split(grad), split(gen_ref[...]), (((1,), (0,)), ((), ())))
    rows, cols = packed_ref.shape
    packed_ref[nact:, :] = jnp.zeros((rows - nact, cols), jnp.float32) + jnp.sum(grad * grad)


def general_kernel(grad_ref, act_ref, out_ref):
    out_ref[...] = product(split(grad_ref[...].T), split(act_ref[...]), (((1,), (0,)), ((), ())))


def scale_kernel(step_scale, whole_scale, a_ref, b_ref, c_ref, d_ref, grad_ref, raw_ref, dir_ref, act_ref, gen_ref):
    total = (a_ref[...] + c_ref[...]) + (b_ref[...] + d_ref[...])
    nact = act_ref.shape[0]
    inverse = 1.0 / jnp.sqrt(total[nact : nact + 1, 0:1] + 1e-06)
    dir_ref[...] = (whole_scale * inverse) * grad_ref[...]
    act_ref[...] = (-step_scale * inverse) * total[:nact]
    gen_ref[...] = (step_scale * inverse) * raw_ref[...]


def tail(tiles, gen_coeffs, act_coeffs, norb):
    nact = act_coeffs.shape[1]
    nbas = gen_coeffs.shape[0]
    f32 = jnp.float32
    shape = jax.ShapeDtypeStruct
    grad, packed = pl.pallas_call(
        grad_kernel, out_shape=(shape((nact, norb), f32), shape((nact + 8, nbas), f32)), compiler_params=SMALL
    )(tiles, gen_coeffs.T)
    raw = pl.pallas_call(general_kernel, out_shape=shape((norb, nbas), f32), compiler_params=SMALL)(grad, act_coeffs.T)
    packed = packed + swap_core(packed)
    others = [swap(packed, X, NX, mask) for mask in (1, 2, 3)]
    direction, active, general = pl.pallas_call(
        functools.partial(scale_kernel, math.sqrt(nact), math.sqrt(nact * norb * 2 * NX)),
        out_shape=(shape((nact, norb), f32), shape((nact, nbas), f32), shape((norb, nbas), f32)),
        compiler_params=SMALL,
    )(packed, *others, grad, raw)
    return direction, active.T, general.T


def on_device(pair_coeffs, rdm, b_tensor, gen_coeffs, act_coeffs):
    naux, nact, norb = b_tensor.shape
    half = naux // 2
    rows = [rdm, swap(rdm, "y", NY, 1)]
    near = {0: pair_coeffs}
    far = {0: swap(pair_coeffs, "y", NY, 3)}
    far[1], far[7] = shift(far[0], "z", NZ, -1), shift(far[0], "z", NZ, 1)
    for k in range(1, NZ // 2):
        near[k] = shift(near[k - 1], "z", NZ, -1)
        near[NZ - k] = shift(near[(NZ - k + 1) % NZ], "z", NZ, 1)
    near[4] = shift(near[3], "z", NZ, -1)
    for k in (2, 6, 3, 5, 4):
        far[k] = swap(near[k], "y", NY, 3)

    kept, sent, *rows = pair_product([near[k] for k in range(NZ)], rows, True)
    chunks = [kept, swap_core(sent)]
    kept, sent = pair_product([far[(k + TURN) % NZ] for k in range(NZ)], rows, False)
    chunks += [kept, swap_core(sent)]
    first, second = sum_over_x(chunks)

    def rank(yy, zz, xx, cc):
        return (((yy * NZ + zz % NZ) * 2 + xx // 2) * 2 + cc) * 2 + xx % 2

    def send_home(value, mask, turn):
        pairs = [
            (rank(yy, zz, xx, cc), rank(yy ^ mask, zz + xx + NX * cc + turn, xx, cc))
            for yy in range(NY)
            for zz in range(NZ)
            for xx in range(NX)
            for cc in range(2)
        ]
        return lax.ppermute(value, ("y", "z", "xh", "co", "xl"), pairs)

    returned = pl.pallas_call(
        lanes_kernel,
        out_shape=jax.ShapeDtypeStruct((naux, 2 * first.shape[1]), first.dtype),
        compiler_params=SMALL,
    )(send_home(first, 0, 0), send_home(second, 3, TURN))

    after = shift(returned, X, NX, -1)
    before = shift(returned, X, NX, 1)
    far_low = shift(after[:half], X, NX, -1)
    far_high = shift(before[half:], X, NX, 1)
    mine = [[returned], [after], [far_low, far_high], [before]]
    theirs = [[swap_core(piece) for piece in group] for group in mine]

    lanes = 128 if norb > 128 else norb // NX
    tiles = fock_product(mine + theirs, b_tensor, lanes)
    piece = jnp.sum(lax.all_to_all(tiles, "z", split_axis=0, concat_axis=0, tiled=True), axis=0)
    piece = (piece + swap(piece, "y", NY, 2)) + (swap(piece, "y", NY, 1) + swap(piece, "y", NY, 3))
    tiles = lax.all_to_all(
        jnp.broadcast_to(piece[None], tiles.shape), "z", split_axis=0, concat_axis=0, tiled=True
    )
    return tail(tiles, gen_coeffs, act_coeffs, norb)


def solution(mesh):
    grid = Mesh(mesh.devices.reshape(NY, NZ, 2, 2, 2), ("y", "z", "xh", "co", "xl"))
    aux, cols = ("y", "z"), ("xh", "co", "xl")
    return jax.shard_map(
        on_device,
        mesh=grid,
        in_specs=(P(aux, cols), P(aux, cols), P(aux, None, cols), P(aux, cols), P(aux, None)),
        out_specs=(P(None, cols), P(aux, None), P(aux, cols)),
        check_vma=False,
    )
```

```python
import functools
import math

import jax
import jax.numpy as jnp
from jax import lax
from jax.experimental import pallas as pl
from jax.experimental.pallas import tpu as pltpu
from jax.sharding import Mesh, PartitionSpec as P

NY, NZ, NX = 4, 8, 4
TURN = 2
X = ("xh", "xl")
SMALL = pltpu.CompilerParams(vmem_limit_bytes=8 * 2**20)


def shift(value, axis, size, step):
    return lax.ppermute(value, axis, [(i, (i + step) % size) for i in range(size)])


def swap_core(value):
    return lax.ppermute(value, "co", [(0, 1), (1, 0)])


def swap(value, axis, size, mask):
    return lax.ppermute(value, axis, [(i, i ^ mask) for i in range(size)])


def split(value):
    head = value.astype(jnp.bfloat16)
    return head, (value - head.astype(jnp.float32)).astype(jnp.bfloat16)


def position():
    return lax.axis_index("y"), lax.axis_index("z"), lax.axis_index("xh") * 2 + lax.axis_index("xl"), lax.axis_index("co")


def product(left, right, dims):
    head, rest = left
    first, second = right
    total = lax.dot_general(head, first, dims, preferred_element_type=jnp.float32)
    total += lax.dot_general(head, second, dims, preferred_element_type=jnp.float32)
    return total + lax.dot_general(rest, first, dims, preferred_element_type=jnp.float32)


def pair_kernel(n_p, fresh, *refs):
    p_both = refs[-1]
    p_refs = refs[:n_p]
    if fresh:
        r_refs, (kept_ref, sent_ref, r_head, r_rest) = refs[n_p:-5], refs[-5:-1]
        start = 0
        for ref in r_refs:
            rows = ref.shape[0]
            r_head[start : start + rows, :], r_rest[start : start + rows, :] = split(ref[...])
            start += rows
    else:
        r_head, r_rest, kept_ref, sent_ref = refs[n_p:-1]
    _, _, x, core = position()
    half, n_cols = kept_ref.shape
    for k, ref in enumerate(p_refs):
        rows = ref.shape[0]
        start = ((k // NX) ^ core) * half + ((k % NX - x) & (NX - 1)) * rows
        start = pl.multiple_of(start, 16)
        p_both[pl.ds(start, rows), :], p_both[pl.ds(start + 2 * half, rows), :] = split(ref[...])
    for low in range(0, n_cols, 256):
        high = min(low + 256, n_cols)
        dims = (((1,), (1,)), ((), ()))
        both = lax.dot_general(p_both[...], r_head[low:high, :], dims, preferred_element_type=jnp.float32)
        cross = lax.dot_general(p_both[: 2 * half], r_rest[low:high, :], dims, preferred_element_type=jnp.float32)
        total = both[: 2 * half] + (both[2 * half :] + cross)
        kept_ref[:, low:high] = total[:half]
        sent_ref[:, low:high] = total[half:]


def pair_product(p_pieces, rows, fresh):
    depth = p_pieces[0].shape[1]
    n_rows = sum(p.shape[0] for p in p_pieces)
    n_cols = sum(r.shape[0] for r in rows) if fresh else rows[0].shape[0]
    shape = jax.ShapeDtypeStruct((n_rows // 2, n_cols), jnp.float32)
    parts = jax.ShapeDtypeStruct((n_cols, depth), jnp.bfloat16)
    return pl.pallas_call(
        functools.partial(pair_kernel, len(p_pieces), fresh),
        out_shape=(shape, shape) + ((parts, parts) if fresh else ()),
        scratch_shapes=[pltpu.VMEM((2 * n_rows, depth), jnp.bfloat16)],
        compiler_params=pltpu.CompilerParams(vmem_limit_bytes=16 * 2**20),
        cost_estimate=pl.CostEstimate(
            flops=1000 if fresh else 6 * n_rows * n_cols * depth,
            bytes_accessed=1000 if fresh else 4 * (n_rows + n_cols) * depth,
            transcendentals=0,
        ),
    )(*p_pieces, *rows)


def join_kernel(*refs):
    chunks, (own_ref, after_ref, before_ref, low_ref, high_ref) = refs[:-5], refs[-5:]
    rows = own_ref.shape[0]
    start = 0
    for kept_ref, got_ref in zip(chunks[::2], chunks[1::2]):
        lanes = slice(start, start + kept_ref.shape[1])
        start = lanes.stop
        total = kept_ref[...] + got_ref[...]
        own_ref[:, lanes] = total[:rows]
        after_ref[:, lanes] = total[rows : 2 * rows]
        low_ref[:, lanes] = total[2 * rows : 2 * rows + rows // 2]
        high_ref[:, lanes] = total[2 * rows + rows // 2 : 3 * rows]
        before_ref[:, lanes] = total[3 * rows :]


def add_kernel(after_ref, up_ref, before_ref, down_ref, after_out, before_out):
    half = up_ref.shape[0]
    after_out[:half] = after_ref[:half] + up_ref[...]
    after_out[half:] = after_ref[half:]
    before_out[:half] = before_ref[:half]
    before_out[half:] = before_ref[half:] + down_ref[...]


def sides_kernel(own_ref, one_ref, two_ref, first_ref, second_ref):
    total = own_ref[...] + one_ref[...] + two_ref[...]
    lanes = first_ref.shape[1]
    first_ref[...] = total[:, :lanes]
    second_ref[...] = total[:, lanes:]


def lanes_kernel(first_ref, second_ref, out_ref):
    lanes = first_ref.shape[1]
    out_ref[:, :lanes] = first_ref[...]
    out_ref[:, lanes:] = second_ref[...]


def sum_over_x(chunks):
    rows = chunks[0].shape[0] // NX
    lanes = sum(chunk.shape[1] for chunk in chunks[::2])
    whole, part = (jax.ShapeDtypeStruct((n, lanes), jnp.float32) for n in (rows, rows // 2))
    own, after, before, low, high = pl.pallas_call(
        join_kernel, out_shape=(whole, whole, whole, part, part), compiler_params=SMALL
    )(*chunks)
    up, down = shift(low, X, NX, 1), shift(high, X, NX, -1)
    after, before = pl.pallas_call(add_kernel, out_shape=(whole, whole), compiler_params=SMALL)(after, up, before, down)
    side = jax.ShapeDtypeStruct((rows, lanes // 2), jnp.float32)
    return pl.pallas_call(sides_kernel, out_shape=(side, side), compiler_params=SMALL)(
        own, shift(after, X, NX, 1), shift(before, X, NX, -1)
    )


def fock_kernel(sizes, nact, per_step, *refs):
    b_ref, out_ref, sorted_ref, acc_ref = refs[-4:]
    y, z, x, core = position()
    naux = b_ref.shape[0]
    steps = naux // per_step

    n_t = refs[0].shape[1] // nact // NY
    at = 0
    for g, size in enumerate(sizes):
        c, s = g // NX, g % NX
        zb = (z - ((x + s) & (NX - 1)) - NX * ((core + c) & 1)) & (NZ - 1)
        base = 0
        for ref in refs[at : at + size]:
            rows = ref.shape[0]
            for j, mask in enumerate((0, 1, 3, 2)):
                turned = zb if j < 2 else (zb - TURN) & (NZ - 1)
                first = ((y ^ mask) * NZ + turned) * n_t
                for t in range(n_t):
                    place = pl.ds(pl.multiple_of((first + t) * naux + base, 8), rows)
                    low = (j * n_t + t) * nact
                    sorted_ref[place, :] = ref[:, low : low + nact]
            base += rows
        at += size
    acc_ref[...] = jnp.zeros_like(acc_ref)

    def step(i, carry):
        total = acc_ref[...]
        for j in range(0, per_step, 2):
            q = i * per_step + j
            left = [sorted_ref[pl.ds(q + side, nact, stride=naux), :] for side in range(2)]
            head, rest = split(jnp.concatenate(left, axis=1))
            b_head, b_rest = split(b_ref[pl.ds(q, 2)].reshape(2 * nact, b_ref.shape[2]))
            both = jnp.dot(jnp.concatenate([head, rest]), b_head, preferred_element_type=jnp.float32)
            total += jnp.dot(head, b_rest, preferred_element_type=jnp.float32) + both[:nact] + both[nact:]
        acc_ref[...] = total
        return carry

    lax.fori_loop(0, steps, step, 0)
    half, lanes = out_ref.shape[1:]
    norb = acc_ref.shape[1]
    for h in range(2):
        for j in range(NX):
            wide = min(lanes, norb - j * lanes)
            if wide < lanes:
                out_ref[h * NX + j] = jnp.zeros((half, lanes), jnp.float32)
            out_ref[h * NX + j, :, :wide] = acc_ref[h * half : (h + 1) * half, j * lanes : j * lanes + wide]


def fock_product(fitted, b_tensor, lanes):
    naux, nact, norb = b_tensor.shape
    per_step = 8
    flat = [piece for group in fitted for piece in group]
    vmem = pl.BlockSpec(memory_space=pltpu.VMEM)
    return pl.pallas_call(
        functools.partial(fock_kernel, [len(group) for group in fitted], nact, per_step),
        out_shape=jax.ShapeDtypeStruct((2 * NX, nact // 2, lanes), jnp.float32),
        in_specs=[vmem] * (len(flat) + 1),
        out_specs=vmem,
        scratch_shapes=[
            pltpu.VMEM((nact * naux, nact), jnp.float32),
            pltpu.VMEM((nact, norb), jnp.float32),
        ],
        compiler_params=pltpu.CompilerParams(vmem_limit_bytes=16 * 2**20),
    )(*flat, b_tensor)


def grad_kernel(tiles_ref, gen_ref, grad_ref, packed_ref):
    half, lanes = tiles_ref.shape[1:]
    nact, norb = grad_ref.shape
    for h in range(2):
        for j in range(NX):
            wide = min(lanes, norb - j * lanes)
            grad_ref[h * half : (h + 1) * half, j * lanes : j * lanes + wide] = 2.0 * tiles_ref[h * NX + j, :, :wide]
    grad = grad_ref[...]
    packed_ref[:nact, :] = product(split(grad), split(gen_ref[...]), (((1,), (0,)), ((), ())))
    rows, cols = packed_ref.shape
    packed_ref[nact:, :] = jnp.zeros((rows - nact, cols), jnp.float32) + jnp.sum(grad * grad)


def general_kernel(grad_ref, act_ref, out_ref):
    out_ref[...] = product(split(grad_ref[...].T), split(act_ref[...]), (((1,), (0,)), ((), ())))


def scale_kernel(step_scale, whole_scale, a_ref, b_ref, c_ref, d_ref, grad_ref, raw_ref, dir_ref, act_ref, gen_ref):
    total = (a_ref[...] + c_ref[...]) + (b_ref[...] + d_ref[...])
    nact = act_ref.shape[0]
    inverse = 1.0 / jnp.sqrt(total[nact : nact + 1, 0:1] + 1e-06)
    dir_ref[...] = (whole_scale * inverse) * grad_ref[...]
    act_ref[...] = (-step_scale * inverse) * total[:nact]
    gen_ref[...] = (step_scale * inverse) * raw_ref[...]


def tail(tiles, gen_coeffs, act_coeffs, norb):
    nact = act_coeffs.shape[1]
    nbas = gen_coeffs.shape[0]
    f32 = jnp.float32
    shape = jax.ShapeDtypeStruct
    grad, packed = pl.pallas_call(
        grad_kernel, out_shape=(shape((nact, norb), f32), shape((nact + 8, nbas), f32)), compiler_params=SMALL
    )(tiles, gen_coeffs.T)
    raw = pl.pallas_call(general_kernel, out_shape=shape((norb, nbas), f32), compiler_params=SMALL)(grad, act_coeffs.T)
    packed = packed + swap_core(packed)
    others = [swap(packed, X, NX, mask) for mask in (1, 2, 3)]
    direction, active, general = pl.pallas_call(
        functools.partial(scale_kernel, math.sqrt(nact), math.sqrt(nact * norb * 2 * NX)),
        out_shape=(shape((nact, norb), f32), shape((nact, nbas), f32), shape((norb, nbas), f32)),
        compiler_params=SMALL,
    )(packed, *others, grad, raw)
    return direction, active.T, general.T


def on_device(pair_coeffs, rdm, b_tensor, gen_coeffs, act_coeffs):
    naux, nact, norb = b_tensor.shape
    half = naux // 2
    rows = [rdm, swap(rdm, "y", NY, 1)]
    near = {0: pair_coeffs}
    far = {0: swap(pair_coeffs, "y", NY, 3)}
    for k in range(1, NZ // 2):
        for found in (near, far):
            if found is near or k < 3:
                found[k] = shift(found[k - 1], "z", NZ, -1)
                found[NZ - k] = shift(found[(NZ - k + 1) % NZ], "z", NZ, 1)
    near[4] = shift(near[3], "z", NZ, -1)
    for k in (3, 5, 4):
        far[k] = swap(near[k], "y", NY, 3)

    kept, sent, *rows = pair_product([near[k] for k in range(NZ)], rows, True)
    chunks = [kept, swap_core(sent)]
    kept, sent = pair_product([far[(k + TURN) % NZ] for k in range(NZ)], rows, False)
    chunks += [kept, swap_core(sent)]
    first, second = sum_over_x(chunks)

    def rank(yy, zz, xx, cc):
        return (((yy * NZ + zz % NZ) * 2 + xx // 2) * 2 + cc) * 2 + xx % 2

    def send_home(value, mask, turn):
        pairs = [
            (rank(yy, zz, xx, cc), rank(yy ^ mask, zz + xx + NX * cc + turn, xx, cc))
            for yy in range(NY)
            for zz in range(NZ)
            for xx in range(NX)
            for cc in range(2)
        ]
        return lax.ppermute(value, ("y", "z", "xh", "co", "xl"), pairs)

    returned = pl.pallas_call(
        lanes_kernel,
        out_shape=jax.ShapeDtypeStruct((naux, 2 * first.shape[1]), first.dtype),
        compiler_params=SMALL,
    )(send_home(first, 0, 0), send_home(second, 3, TURN))

    after = shift(returned, X, NX, -1)
    before = shift(returned, X, NX, 1)
    far_low = shift(after[:half], X, NX, -1)
    far_high = shift(before[half:], X, NX, 1)
    mine = [[returned], [after], [far_low, far_high], [before]]
    theirs = [[swap_core(piece) for piece in group] for group in mine]

    lanes = 128 if norb > 128 else norb // NX
    tiles = fock_product(mine + theirs, b_tensor, lanes)
    piece = jnp.sum(lax.all_to_all(tiles, "z", split_axis=0, concat_axis=0, tiled=True), axis=0)
    piece = (piece + swap(piece, "y", NY, 2)) + (swap(piece, "y", NY, 1) + swap(piece, "y", NY, 3))
    tiles = lax.all_to_all(
        jnp.broadcast_to(piece[None], tiles.shape), "z", split_axis=0, concat_axis=0, tiled=True
    )
    return tail(tiles, gen_coeffs, act_coeffs, norb)


def solution(mesh):
    grid = Mesh(mesh.devices.reshape(NY, NZ, 2, 2, 2), ("y", "z", "xh", "co", "xl"))
    aux, cols = ("y", "z"), ("xh", "co", "xl")
    return jax.shard_map(
        on_device,
        mesh=grid,
        in_specs=(P(aux, cols), P(aux, cols), P(aux, None, cols), P(aux, cols), P(aux, None)),
        out_specs=(P(None, cols), P(aux, None), P(aux, cols)),
        check_vma=False,
    )
```
